256 devices in a mesh: dp: 2 (over x_hi), gx: 16 (over z, core), gy: 8 (over y, x_lo).
Axes of the slice: x: 4 (x_hi: 2, x_lo: 2; x = x_hi * 2 + x_lo), y: 4, z: 8, core: 2. Of those that a mesh axis runs over, the one named last changes fastest.
Arguments:
- activations: bfloat16 [2, 32, 64, 128, 128], P('dp', None, 'gx', 'gy'), may hold values from -6 to 6
- kernel: bfloat16 [64, 32, 3, 3, 3], replicated, may hold values from -0.21875 to 0.21875
- out_grad: bfloat16 [2, 64, 64, 128, 128], P('dp', None, 'gx', 'gy'), may hold values from -6 to 6
Outputs:
- output: bfloat16 [2, 64, 64, 128, 128], P('dp', None, 'gx', 'gy')
- in_grad: bfloat16 [2, 32, 64, 128, 128], P('dp', None, 'gx', 'gy')
- kernel_grad: float32 [64, 32, 3, 3, 3], replicated
The draws below stay inside these ranges and needn't reach their ends.
All inputs are finite; a program needn't handle non-finite values.
Results may differ from the reference program's by a relative error of at most 0.0014.
Values may be sent and summed in bfloat16 or wider, within the bound.
A program may use at most 64 MiB of HBM per device.

```python
import math
import jax
import jax.numpy as jnp
from jax import lax

CIN = 32
COUT = 64
NZ = 128
UNIV = 2
NX = 64
NY = 128


def block_scale(own_key, shape, cuts, low, top_value):
    factor_of = 1.0
    for position, shards_of in cuts:
        steps = jax.random.uniform(jax.random.fold_in(jax.random.fold_in(own_key, 6), position), (shards_of,), jnp.float32, low / len(cuts), top_value / len(cuts))
        factor_of = factor_of * jnp.repeat(jnp.exp(steps), shape[position] // shards_of).reshape((-1,) + (1,) * (len(shape) - 1 - position))
    return factor_of


def scatter_about(own_key, shape, deviation, limit, split=(), held_as=jnp.bfloat16):
    factor_of = block_scale(own_key, shape, split, -0.22, 0.18) if split else 1.0
    drawn = jax.random.normal(own_key, shape, jnp.float32) * deviation * factor_of
    return jnp.minimum(jnp.maximum(drawn, -limit), limit).astype(held_as)


def setup_inputs(seed: int = 0) -> dict:
    seeds = jax.random.split(jax.random.key(seed), 4)
    activations = scatter_about(seeds[0], (UNIV, CIN, NX, NY, NZ), 1.0, 6.0, ((0, 2), (2, 16), (3, 8)))
    kernel = scatter_about(seeds[1], (COUT, CIN, 3, 3, 3), (27 * CIN) ** -0.5, 0.21875)
    out_grad = scatter_about(seeds[2], (UNIV, COUT, NX, NY, NZ), 1.0, 6.0, ((0, 2), (2, 16), (3, 8)))
    return {"activations": activations, "kernel": kernel, "out_grad": out_grad}


def periodic(field):
    return jnp.pad(field, ((0, 0), (0, 0), (1, 1), (1, 1), (1, 1)), mode='wrap')

def forward_conv(padded, weights):
    return lax.conv_general_dilated(padded, weights, (1, 1, 1), 'VALID', dimension_numbers=('NCDHW', 'OIDHW', 'NCDHW'), preferred_element_type=jnp.float32)

def weight_conv(padded, cotangent):
    return lax.conv_general_dilated(padded, cotangent, (1, 1, 1), 'VALID', dimension_numbers=('CNDHW', 'IODHW', 'CNDHW'), preferred_element_type=jnp.float32)

def reference(activations, kernel, out_grad):
    padded = periodic(activations)
    output = forward_conv(padded, kernel).astype(jnp.bfloat16)
    flipped = jnp.flip(kernel, (2, 3, 4)).transpose(1, 0, 2, 3, 4)
    in_grad = forward_conv(periodic(out_grad), flipped).astype(jnp.bfloat16)
    total = UNIV * NX * NY * NZ
    kernel_grad = weight_conv(padded, out_grad) * jnp.float32(1.0 / math.sqrt(total))
    return (output, in_grad, kernel_grad)
```

```python
import functools
import math

import jax
import jax.numpy as jnp
from jax import lax
from jax.experimental import pallas as pl
from jax.experimental.pallas import tpu as pltpu
from jax.sharding import PartitionSpec as P

MESH = pl.DeviceIdType.MESH
LANES = 128
AROUND = [(-1, 0), (1, 0), (0, -1), (0, 1), (-1, -1), (-1, 1), (1, -1), (1, 1)]


def kernel(sizes, scale, act_hbm, w_ref, og_hbm, out_hbm, ing_hbm, kg_ref,
           act_v, og_v, act_e, og_e, og_r, stage, w_fwd, w_bwd, grad, dense, slots, near, sums, zed, gathered, full,
           out_v, ing_v, in_sem, out_sem, ha_send, ha_recv, ho_send, ho_recv,
           p1_send, p1_recv, p2_send, p2_recv, p3_send, p3_recv, p4_send, p4_recv, p5_send, p5_recv):
    n_dp, n_gx, n_gy = sizes
    cin, ni, nj, _ = act_v.shape
    cout = og_v.shape[0]
    nz = n_gx // 2
    group = n_dp * n_gy
    dp, gx, gy = lax.axis_index("dp"), lax.axis_index("gx"), lax.axis_index("gy")
    z, core = lax.div(gx, 2), lax.rem(gx, 2)
    place = dp * n_gy + gy

    def shifted(di, dj):
        return (dp, lax.rem(gx + di + n_gx, n_gx), lax.rem(gy + dj + n_gy, n_gy))

    def along_z(dz):
        return (dp, lax.rem(z + dz, nz) * 2 + core, gy)

    other_core = (dp, z * 2 + 1 - core, gy)

    def across(d):
        peer = lax.rem(place + d, group)
        return (lax.div(peer, n_gy), gx, lax.rem(peer, n_gy))

    act_in = pltpu.make_async_copy(act_hbm, act_v, in_sem.at[0])
    og_in = pltpu.make_async_copy(og_hbm, og_v, in_sem.at[1])
    act_in.start()
    og_in.start()

    barrier = pltpu.get_barrier_semaphore()

    def greet(target):
        pl.semaphore_signal(barrier, inc=1, device_id=target, device_id_type=MESH)

    for di, dj in AROUND:
        if di:
            greet(shifted(di, dj))
    lax.fori_loop(1, nz, lambda d, c: (greet(along_z(d)), c)[1], 0)
    lax.fori_loop(1, group, lambda d, c: (greet(across(d)), c)[1], 0)

    def halo(field, n, send, recv):
        di, dj = AROUND[n]
        rows = {-1: (1, ni + 1, 1), 0: (1, 1, ni), 1: (ni, 0, 1)}[di]
        cols = {-1: (1, nj + 1, 1), 0: (1, 1, nj), 1: (nj, 0, 1)}[dj]
        return pltpu.make_async_remote_copy(
            src_ref=field.at[pl.ds(rows[0], rows[2]), :, pl.ds(cols[0] * LANES, cols[2] * LANES)],
            dst_ref=field.at[pl.ds(rows[1], rows[2]), :, pl.ds(cols[1] * LANES, cols[2] * LANES)],
            send_sem=send.at[n],
            recv_sem=recv.at[n],
            device_id=shifted(di, dj),
            device_id_type=MESH,
        )

    act_in.wait()

    def turn_act(i, carry):
        stage[pl.ds(0, cin * nj)] = act_v[:, i].astype(jnp.float32).reshape(cin * nj, LANES)
        for j in range(nj):
            act_e[i + 1, :, pl.ds((j + 1) * LANES, LANES)] = stage[pl.ds(j, cin, stride=nj)].astype(jnp.bfloat16)
        return carry

    lax.fori_loop(0, ni, turn_act, 0)
    pl.semaphore_wait(barrier, 6 + (nz - 1) + (group - 1))
    for n in range(8):
        halo(act_e, n, ha_send, ha_recv).start()

    og_in.wait()

    def turn_og(i, carry):
        stage[...] = og_v[:, i].astype(jnp.float32).reshape(cout * nj, LANES)
        for j in range(nj):
            rows = stage[pl.ds(j, cout, stride=nj)]
            at = pl.ds(j * LANES, LANES)
            og_e[i + 1, :, pl.ds((j + 1) * LANES, LANES)] = rows.astype(jnp.bfloat16)
            og_r[i, pl.ds(0, cout), at] = pltpu.roll(rows, LANES - 1, 1).astype(jnp.bfloat16)
            og_r[i, pl.ds(cout, cout), at] = rows.astype(jnp.bfloat16)
            og_r[i, pl.ds(2 * cout, cout), at] = pltpu.roll(rows, 1, 1).astype(jnp.bfloat16)
        return carry

    lax.fori_loop(0, ni, turn_og, 0)
    for n in range(8):
        halo(og_e, n, ho_send, ho_recv).start()

    w = w_ref[...].astype(jnp.float32).reshape(9, 3, cin, cout)
    by_tap = jnp.concatenate([w[:, e].reshape(9 * cin, cout) for e in range(3)], axis=1)
    w_fwd[...] = by_tap.T.astype(jnp.bfloat16)
    w_bwd[...] = jnp.concatenate([w[n].reshape(3 * cin, cout) for n in range(9)], axis=1).astype(jnp.bfloat16)

    for n in range(8):
        halo(act_e, n, ha_send, ha_recv).wait_recv()

    grad[...] = jnp.zeros_like(grad)

    def weight_term(i, carry):
        taps = jnp.concatenate(
            [act_e[i + a, :, pl.ds(b * LANES, nj * LANES)] for a in range(3) for b in range(3)], axis=0
        )
        grad[...] += lax.dot_general(taps, og_r[i], (((1,), (1,)), ((), ())), preferred_element_type=jnp.float32)
        return carry

    lax.fori_loop(0, ni, weight_term, 0)
    tall = 9 * cin
    half = tall // 2
    dense[pl.ds(0, tall)] = grad[:, :LANES]
    dense[pl.ds(tall, half)] = jnp.concatenate([grad[:half, LANES:], grad[half:, LANES:]], axis=1)
    part = slots.shape[2]
    for s in range(n_gx):
        slots[s // nz, s % nz] = dense[pl.ds(s * part, part)]

    def forward(i):
        def chunk(p, carry):
            taps = jnp.concatenate(
                [
                    act_e[i + a, :, pl.ds(pl.multiple_of((2 * p + b) * LANES, LANES), 2 * LANES)]
                    for a in range(3)
                    for b in range(3)
                ],
                axis=0,
            )
            y = jnp.dot(w_fwd[...], taps, preferred_element_type=jnp.float32)
            for q in range(2):
                t = y[:, q * LANES : (q + 1) * LANES]
                total = t[cout : 2 * cout] + pltpu.roll(t[:cout], 1, 1) + pltpu.roll(t[2 * cout :], LANES - 1, 1)
                stage[pl.ds(2 * p + q, cout, stride=nj)] = total
            return carry

        lax.fori_loop(0, nj // 2, chunk, 0)
        out_v[i] = stage[...].astype(jnp.bfloat16).reshape(cout, nj, LANES)
        pltpu.make_async_copy(out_v.at[i], out_hbm.at[:, i], out_sem.at[i]).start()

    def backward(i):
        def chunk(p, carry):
            taps = jnp.concatenate(
                [
                    og_e[i + 2 - a, :, pl.ds(pl.multiple_of((2 * p + 2 - b) * LANES, LANES), 2 * LANES)]
                    for a in range(3)
                    for b in range(3)
                ],
                axis=0,
            )
            y = jnp.dot(w_bwd[...], taps, preferred_element_type=jnp.float32)
            for q in range(2):
                t = y[:, q * LANES : (q + 1) * LANES]
                total = t[cin : 2 * cin] + pltpu.roll(t[:cin], LANES - 1, 1) + pltpu.roll(t[2 * cin :], 1, 1)
                stage[pl.ds(2 * p + q, cin, stride=nj)] = total
            return carry

        lax.fori_loop(0, nj // 2, chunk, 0)
        ing_v[i] = stage[pl.ds(0, cin * nj)].astype(jnp.bfloat16).reshape(cin, nj, LANES)
        pltpu.make_async_copy(ing_v.at[i], ing_hbm.at[:, i], out_sem.at[ni + i]).start()

    def far_first(t):
        return nz // 2 + lax.div(t + 1, 2) * (1 - 2 * lax.rem(t, 2))

    def to_core(dz):
        at = lax.rem(z + dz, nz)
        return pltpu.make_async_remote_copy(
            src_ref=slots.at[1 - core, at], dst_ref=near.at[at], send_sem=p1_send.at[dz], recv_sem=p1_recv.at[dz],
            device_id=other_core, device_id_type=MESH)

    def to_z(dz):
        return pltpu.make_async_remote_copy(
            src_ref=sums.at[dz], dst_ref=zed.at[dz], send_sem=p2_send.at[dz], recv_sem=p2_recv.at[dz],
            device_id=along_z(dz), device_id_type=MESH)

    def to_group(d):
        return pltpu.make_async_remote_copy(
            src_ref=gathered.at[place], dst_ref=gathered.at[place], send_sem=p3_send.at[d], recv_sem=p3_recv.at[d],
            device_id=across(d), device_id_type=MESH)

    def back_z(dz):
        return pltpu.make_async_remote_copy(
            src_ref=full.at[core, z], dst_ref=full.at[core, z], send_sem=p4_send.at[dz], recv_sem=p4_recv.at[dz],
            device_id=along_z(dz), device_id_type=MESH)

    def back_core(dz):
        at = lax.rem(z - dz + nz, nz)
        return pltpu.make_async_remote_copy(
            src_ref=full.at[core, at], dst_ref=full.at[core, at], send_sem=p5_send.at[dz], recv_sem=p5_recv.at[dz],
            device_id=other_core, device_id_type=MESH)

    def each(low, high, do):
        def body(t, carry):
            do(t)
            return carry

        lax.fori_loop(low, high, body, 0)

    each(0, nz, lambda t: to_core(far_first(t)).start())
    each(0, 1, forward)

    def pass_z(t):
        dz = far_first(t)
        to_core(dz).wait_recv()
        at = lax.rem(z + dz, nz)
        sums[dz] = slots[core, at] + near[at]

    def send_z(t):
        pass_z(t)
        to_z(far_first(t)).start()

    each(0, nz - 1, send_z)
    pass_z(nz - 1)
    each(1, 3, forward)
    each(1, nz, lambda dz: to_z(dz).wait_recv())
    total = sums[0]
    for dz in range(1, nz):
        total = total + zed[dz]
    gathered[place] = total
    each(1, group, lambda d: to_group(d).start())
    each(3, ni, forward)
    for n in range(8):
        halo(og_e, n, ho_send, ho_recv).wait_recv()
    each(0, 1, backward)
    each(1, group, lambda d: to_group(d).wait_recv())
    total = gathered[0]
    for p in range(1, group):
        total = total + gathered[p]
    full[core, z] = total * jnp.float32(scale)
    each(1, nz, lambda dz: back_z(dz).start())
    back_core(0).start()
    each(1, 3, backward)

    def forward_core(t):
        dz = t + 1
        back_z(dz).wait_recv()
        back_core(dz).start()

    each(0, nz - 1, forward_core)
    each(3, ni, backward)

    each(0, nz, lambda dz: back_core(dz).wait_recv())
    for s in range(n_gx):
        dense[pl.ds(s * part, part)] = full[s // nz, s % nz]
    for n in range(9):
        rows = pl.ds(n * cin, cin)
        kg_ref[pl.ds(n * 3 * cin, cin)] = dense[rows, pl.ds(0, cout)]
        kg_ref[pl.ds((n * 3 + 1) * cin, cin)] = dense[rows, pl.ds(cout, cout)]
    third = jnp.concatenate([dense[pl.ds(tall, half), :cout], dense[pl.ds(tall, half), cout:]], axis=0)
    for n in range(9):
        kg_ref[pl.ds((n * 3 + 2) * cin, cin)] = third[n * cin : (n + 1) * cin]

    for n in range(8):
        halo(act_e, n, ha_send, ha_recv).wait_send()
        halo(og_e, n, ho_send, ho_recv).wait_send()
    each(0, nz, lambda dz: to_core(dz).wait_send())
    each(1, nz, lambda dz: to_z(dz).wait_send())
    each(1, group, lambda d: to_group(d).wait_send())
    each(1, nz, lambda dz: back_z(dz).wait_send())
    each(0, nz, lambda dz: back_core(dz).wait_send())
    each(0, ni, lambda i: pltpu.make_async_copy(out_v.at[i], out_hbm.at[:, i], out_sem.at[i]).wait())
    each(0, ni, lambda i: pltpu.make_async_copy(ing_v.at[i], ing_hbm.at[:, i], out_sem.at[ni + i]).wait())


def local(sizes, activations, weights, out_grad):
    n_dp, n_gx, n_gy = sizes
    univ, cin, ni, nj, nk = activations.shape
    cout = out_grad.shape[1]
    nz, group = n_gx // 2, n_dp * n_gy
    scale = 1.0 / math.sqrt(univ * n_dp * ni * n_gx * nj * n_gy * nk)
    part = 27 * cin * cout // (LANES * n_gx)
    bf16, f32 = jnp.bfloat16, jnp.float32
    dma = pltpu.SemaphoreType.DMA
    taps = weights.transpose(2, 3, 4, 1, 0).reshape(27 * cin, cout)
    output, in_grad, kernel_grad = pl.pallas_call(
        functools.partial(kernel, sizes, scale),
        out_shape=(
            jax.ShapeDtypeStruct((cout, ni, nj, nk), bf16),
            jax.ShapeDtypeStruct((cin, ni, nj, nk), bf16),
            jax.ShapeDtypeStruct((27 * cin, cout), f32),
        ),
        in_specs=[
            pl.BlockSpec(memory_space=pl.ANY),
            pl.BlockSpec(memory_space=pltpu.VMEM),
            pl.BlockSpec(memory_space=pl.ANY),
        ],
        out_specs=(
            pl.BlockSpec(memory_space=pl.ANY),
            pl.BlockSpec(memory_space=pl.ANY),
            pl.BlockSpec(memory_space=pltpu.VMEM),
        ),
        scratch_shapes=[
            pltpu.VMEM((cin, ni, nj, nk), bf16),
            pltpu.VMEM((cout, ni, nj, nk), bf16),
            pltpu.VMEM((ni + 2, cin, (nj + 2) * nk), bf16),
            pltpu.VMEM((ni + 2, cout, (nj + 2) * nk), bf16),
            pltpu.VMEM((ni, 3 * cout, nj * nk), bf16),
            pltpu.VMEM((cout * nj, nk), f32),
            pltpu.VMEM((3 * cout, 9 * cin), bf16),
            pltpu.VMEM((3 * cin, 9 * cout), bf16),
            pltpu.VMEM((9 * cin, 3 * cout), f32),
            pltpu.VMEM((part * n_gx, LANES), f32),
            pltpu.VMEM((2, nz, part, LANES), f32),
            pltpu.VMEM((nz, part, LANES), f32),
            pltpu.VMEM((nz, part, LANES), f32),
            pltpu.VMEM((nz, part, LANES), f32),
            pltpu.VMEM((group, part, LANES), f32),
            pltpu.VMEM((2, nz, part, LANES), f32),
            pltpu.VMEM((ni, cout, nj, nk), bf16),
            pltpu.VMEM((ni, cin, nj, nk), bf16),
            dma((2,)),
            dma((2 * ni,)),
            dma((8,)), dma((8,)), dma((8,)), dma((8,)),
            dma((nz,)), dma((nz,)), dma((nz,)), dma((nz,)),
            dma((group,)), dma((group,)),
            dma((nz,)), dma((nz,)), dma((nz,)), dma((nz,)),
        ],
        compiler_params=pltpu.CompilerParams(
            collective_id=0, has_side_effects=True, vmem_limit_bytes=48 * 1024 * 1024
        ),
        cost_estimate=pl.CostEstimate(flops=3_000_000_000, bytes_accessed=4_000_000, transcendentals=0),
    )(activations[0], taps, out_grad[0])
    kernel_grad = kernel_grad.reshape(3, 3, 3, cin, cout).transpose(4, 3, 0, 1, 2)
    return (output[None], in_grad[None], kernel_grad)


def solution(mesh):
    sizes = (mesh.shape["dp"], mesh.shape["gx"], mesh.shape["gy"])
    return jax.shard_map(
        functools.partial(local, sizes),
        mesh=mesh,
        in_specs=(P("dp", None, "gx", "gy", None), P(), P("dp", None, "gx", "gy", None)),
        out_specs=(P("dp", None, "gx", "gy", None), P("dp", None, "gx", "gy", None), P()),
        check_vma=False,
    )
```

```python
import functools
import math

import jax
import jax.numpy as jnp
from jax import lax
from jax.experimental import pallas as pl
from jax.experimental.pallas import tpu as pltpu
from jax.sharding import PartitionSpec as P

MESH = pl.DeviceIdType.MESH
LANES = 128
AROUND = [(-1, 0), (1, 0), (0, -1), (0, 1), (-1, -1), (-1, 1), (1, -1), (1, 1)]


def kernel(sizes, scale, act_hbm, w_hbm, og_hbm, out_hbm, ing_hbm, kg_ref,
           act_v, w_v, og_v, act_e, og_e, og_r, stage, w_fwd, w_bwd, grad, dense, slots, near, sums, parts, lifted, full,
           out_v, ing_v, in_sem, out_sem, ha_send, ha_recv, ho_send, ho_recv,
           p1_send, p1_recv, p2_send, p2_recv, p3_send, p3_recv, p4_send, p4_recv, p5_send, p5_recv):
    n_dp, n_gx, n_gy = sizes
    cin, ni, nj, _ = act_v.shape
    cout = og_v.shape[0]
    nz = n_gx // 2
    group = n_dp * n_gy
    dp, gx, gy = lax.axis_index("dp"), lax.axis_index("gx"), lax.axis_index("gy")
    z, core = lax.div(gx, 2), lax.rem(gx, 2)
    place = dp * n_gy + gy

    def shifted(di, dj):
        return (dp, lax.rem(gx + di + n_gx, n_gx), lax.rem(gy + dj + n_gy, n_gy))

    def along_z(dz):
        return (dp, lax.rem(z + dz, nz) * 2 + core, gy)

    other_core = (dp, z * 2 + 1 - core, gy)

    def across(d):
        peer = lax.rem(place + d, group)
        return (lax.div(peer, n_gy), gx, lax.rem(peer, n_gy))

    barrier = pltpu.get_barrier_semaphore()

    def greet(target):
        pl.semaphore_signal(barrier, inc=1, device_id=target, device_id_type=MESH)

    for di, dj in AROUND:
        if di:
            greet(shifted(di, dj))
    lax.fori_loop(1, nz, lambda d, c: (greet(along_z(d)), c)[1], 0)
    lax.fori_loop(1, group, lambda d, c: (greet(across(d)), c)[1], 0)

    act_in = pltpu.make_async_copy(act_hbm, act_v, in_sem.at[0])
    og_in = pltpu.make_async_copy(og_hbm, og_v, in_sem.at[1])
    w_in = pltpu.make_async_copy(w_hbm, w_v, in_sem.at[2])
    act_in.start()
    og_in.start()
    w_in.start()

    def halo(field, n, send, recv):
        di, dj = AROUND[n]
        rows = {-1: (1, ni + 1, 1), 0: (1, 1, ni), 1: (ni, 0, 1)}[di]
        cols = {-1: (1, nj + 1, 1), 0: (1, 1, nj), 1: (nj, 0, 1)}[dj]
        return pltpu.make_async_remote_copy(
            src_ref=field.at[pl.ds(rows[0], rows[2]), :, pl.ds(cols[0] * LANES, cols[2] * LANES)],
            dst_ref=field.at[pl.ds(rows[1], rows[2]), :, pl.ds(cols[1] * LANES, cols[2] * LANES)],
            send_sem=send.at[n],
            recv_sem=recv.at[n],
            device_id=shifted(di, dj),
            device_id_type=MESH,
        )

    act_in.wait()

    def turn_act(i, carry):
        stage[pl.ds(0, cin * nj)] = act_v[:, i].astype(jnp.float32).reshape(cin * nj, LANES)
        for j in range(nj):
            act_e[i + 1, :, pl.ds((j + 1) * LANES, LANES)] = stage[pl.ds(j, cin, stride=nj)].astype(jnp.bfloat16)
        return carry

    lax.fori_loop(0, ni, turn_act, 0)
    pl.semaphore_wait(barrier, 6 + (nz - 1) + (group - 1))
    for n in range(8):
        halo(act_e, n, ha_send, ha_recv).start()

    og_in.wait()

    def turn_og(i, carry):
        stage[...] = og_v[:, i].astype(jnp.float32).reshape(cout * nj, LANES)
        for j in range(nj):
            rows = stage[pl.ds(j, cout, stride=nj)]
            at = pl.ds(j * LANES, LANES)
            og_e[i + 1, :, pl.ds((j + 1) * LANES, LANES)] = rows.astype(jnp.bfloat16)
            og_r[i, pl.ds(0, cout), at] = pltpu.roll(rows, LANES - 1, 1).astype(jnp.bfloat16)
            og_r[i, pl.ds(cout, cout), at] = rows.astype(jnp.bfloat16)
            og_r[i, pl.ds(2 * cout, cout), at] = pltpu.roll(rows, 1, 1).astype(jnp.bfloat16)
        return carry

    lax.fori_loop(0, ni, turn_og, 0)
    for n in range(8):
        halo(og_e, n, ho_send, ho_recv).start()

    w_in.wait()
    w = w_v[...].astype(jnp.float32).reshape(9, 3, cin, cout)
    by_tap = jnp.concatenate([w[:, e].reshape(9 * cin, cout) for e in range(3)], axis=1)
    w_fwd[...] = by_tap.T.astype(jnp.bfloat16)
    w_bwd[...] = jnp.concatenate([w[n].reshape(3 * cin, cout) for n in range(9)], axis=1).astype(jnp.bfloat16)

    for n in range(8):
        halo(act_e, n, ha_send, ha_recv).wait_recv()

    grad[...] = jnp.zeros_like(grad)

    def weight_term(i, carry):
        taps = jnp.concatenate(
            [act_e[i + a, :, pl.ds(b * LANES, nj * LANES)] for a in range(3) for b in range(3)], axis=0
        )
        grad[...] += lax.dot_general(taps, og_r[i], (((1,), (1,)), ((), ())), preferred_element_type=jnp.float32)
        return carry

    lax.fori_loop(0, ni, weight_term, 0)
    tall = 9 * cin
    half = tall // 2
    dense[pl.ds(0, tall)] = grad[:, :LANES]
    dense[pl.ds(tall, half)] = jnp.concatenate([grad[:half, LANES:], grad[half:, LANES:]], axis=1)
    part = slots.shape[2]
    extra = 2 * group * part - tall - half
    if extra:
        dense[pl.ds(tall + half, extra)] = jnp.zeros((extra, LANES), jnp.float32)
    for s in range(2 * group):
        slots[s // group, s % group] = dense[pl.ds(s * part, part)]

    def forward(i):
        for p in range(nj // 2):
            taps = jnp.concatenate(
                [
                    act_e[i + a, :, pl.ds((2 * p + b) * LANES, 2 * LANES)]
                    for a in range(3)
                    for b in range(3)
                ],
                axis=0,
            )
            y = jnp.dot(w_fwd[...], taps, preferred_element_type=jnp.float32)
            for q in range(2):
                t = y[:, q * LANES : (q + 1) * LANES]
                total = t[cout : 2 * cout] + pltpu.roll(t[:cout], 1, 1) + pltpu.roll(t[2 * cout :], LANES - 1, 1)
                stage[pl.ds(2 * p + q, cout, stride=nj)] = total
        out_v[i] = stage[...].astype(jnp.bfloat16).reshape(cout, nj, LANES)
        pltpu.make_async_copy(out_v.at[i], out_hbm.at[:, i], out_sem.at[i]).start()

    def backward(i):
        for p in range(nj // 2):
            taps = jnp.concatenate(
                [
                    og_e[i + 2 - a, :, pl.ds((2 * p + 2 - b) * LANES, 2 * LANES)]
                    for a in range(3)
                    for b in range(3)
                ],
                axis=0,
            )
            y = jnp.dot(w_bwd[...], taps, preferred_element_type=jnp.float32)
            for q in range(2):
                t = y[:, q * LANES : (q + 1) * LANES]
                total = t[cin : 2 * cin] + pltpu.roll(t[:cin], LANES - 1, 1) + pltpu.roll(t[2 * cin :], 1, 1)
                stage[pl.ds(2 * p + q, cin, stride=nj)] = total
        ing_v[i] = stage[pl.ds(0, cin * nj)].astype(jnp.bfloat16).reshape(cin, nj, LANES)
        pltpu.make_async_copy(ing_v.at[i], ing_hbm.at[:, i], out_sem.at[ni + i]).start()

    def to_core():
        return pltpu.make_async_remote_copy(
            src_ref=slots.at[1 - core], dst_ref=near, send_sem=p1_send.at[0], recv_sem=p1_recv.at[0],
            device_id=other_core, device_id_type=MESH)

    def to_group(d):
        return pltpu.make_async_remote_copy(
            src_ref=sums.at[lax.rem(place + d, group)], dst_ref=parts.at[place],
            send_sem=p2_send.at[d], recv_sem=p2_recv.at[d], device_id=across(d), device_id_type=MESH)

    def to_z(dz):
        return pltpu.make_async_remote_copy(
            src_ref=lifted.at[z], dst_ref=lifted.at[z], send_sem=p3_send.at[dz], recv_sem=p3_recv.at[dz],
            device_id=along_z(dz), device_id_type=MESH)

    def back_group(d):
        return pltpu.make_async_remote_copy(
            src_ref=full.at[core, place], dst_ref=full.at[core, place], send_sem=p4_send.at[d], recv_sem=p4_recv.at[d],
            device_id=across(d), device_id_type=MESH)

    def back_core(d):
        at = lax.rem(place - d + group, group)
        return pltpu.make_async_remote_copy(
            src_ref=full.at[core, at], dst_ref=full.at[core, at], send_sem=p5_send.at[d], recv_sem=p5_recv.at[d],
            device_id=other_core, device_id_type=MESH)

    def each(low, high, do):
        def body(t, carry):
            do(t)
            return carry

        lax.fori_loop(low, high, body, 0)

    to_core().start()
    to_core().wait_recv()
    sums[...] = slots[core] + near[...]
    each(1, group, lambda d: to_group(d).start())
    parts[place] = sums[place]
    each(0, 2, forward)
    each(1, group, lambda d: to_group(d).wait_recv())
    lifted[z] = jnp.sum(parts[...], axis=0)
    each(1, nz, lambda dz: to_z(dz).start())
    each(2, ni, forward)
    each(1, nz, lambda dz: to_z(dz).wait_recv())
    full[core, place] = jnp.sum(lifted[...], axis=0) * jnp.float32(scale)
    each(1, group, lambda d: back_group(d).start())
    back_core(0).start()
    for n in range(8):
        halo(og_e, n, ho_send, ho_recv).wait_recv()
    each(0, ni, backward)

    def forward_core(t):
        d = t + 1
        back_group(d).wait_recv()
        back_core(d).start()

    each(0, group - 1, forward_core)
    each(0, group, lambda d: back_core(d).wait_recv())
    for s in range(2 * group):
        dense[pl.ds(s * part, part)] = full[s // group, s % group]
    for n in range(9):
        rows = pl.ds(n * cin, cin)
        kg_ref[pl.ds(n * 3 * cin, cin)] = dense[rows, pl.ds(0, cout)]
        kg_ref[pl.ds((n * 3 + 1) * cin, cin)] = dense[rows, pl.ds(cout, cout)]
    third = jnp.concatenate([dense[pl.ds(tall, half), :cout], dense[pl.ds(tall, half), cout:]], axis=0)
    for n in range(9):
        kg_ref[pl.ds((n * 3 + 2) * cin, cin)] = third[n * cin : (n + 1) * cin]

    for n in range(8):
        halo(act_e, n, ha_send, ha_recv).wait_send()
        halo(og_e, n, ho_send, ho_recv).wait_send()
    to_core().wait_send()
    each(1, group, lambda d: to_group(d).wait_send())
    each(1, nz, lambda dz: to_z(dz).wait_send())
    each(1, group, lambda d: back_group(d).wait_send())
    each(0, group, lambda d: back_core(d).wait_send())
    each(0, ni, lambda i: pltpu.make_async_copy(out_v.at[i], out_hbm.at[:, i], out_sem.at[i]).wait())
    each(0, ni, lambda i: pltpu.make_async_copy(ing_v.at[i], ing_hbm.at[:, i], out_sem.at[ni + i]).wait())


def local(sizes, activations, weights, out_grad):
    n_dp, n_gx, n_gy = sizes
    univ, cin, ni, nj, nk = activations.shape
    cout = out_grad.shape[1]
    nz, group = n_gx // 2, n_dp * n_gy
    scale = 1.0 / math.sqrt(univ * n_dp * ni * n_gx * nj * n_gy * nk)
    part = -(-27 * cin * cout // (LANES * 2 * group))
    bf16, f32 = jnp.bfloat16, jnp.float32
    dma = pltpu.SemaphoreType.DMA
    taps = weights.transpose(2, 3, 4, 1, 0).reshape(27 * cin, cout)
    output, in_grad, kernel_grad = pl.pallas_call(
        functools.partial(kernel, sizes, scale),
        out_shape=(
            jax.ShapeDtypeStruct((cout, ni, nj, nk), bf16),
            jax.ShapeDtypeStruct((cin, ni, nj, nk), bf16),
            jax.ShapeDtypeStruct((27 * cin, cout), f32),
        ),
        in_specs=[
            pl.BlockSpec(memory_space=pltpu.HBM),
            pl.BlockSpec(memory_space=pltpu.HBM),
            pl.BlockSpec(memory_space=pltpu.HBM),
        ],
        out_specs=(
            pl.BlockSpec(memory_space=pl.ANY),
            pl.BlockSpec(memory_space=pl.ANY),
            pl.BlockSpec(memory_space=pltpu.VMEM),
        ),
        scratch_shapes=[
            pltpu.VMEM((cin, ni, nj, nk), bf16),
            pltpu.VMEM((27 * cin, cout), bf16),
            pltpu.VMEM((cout, ni, nj, nk), bf16),
            pltpu.VMEM((ni + 2, cin, (nj + 2) * nk), bf16),
            pltpu.VMEM((ni + 2, cout, (nj + 2) * nk), bf16),
            pltpu.VMEM((ni, 3 * cout, nj * nk), bf16),
            pltpu.VMEM((cout * nj, nk), f32),
            pltpu.VMEM((3 * cout, 9 * cin), bf16),
            pltpu.VMEM((3 * cin, 9 * cout), bf16),
            pltpu.VMEM((9 * cin, 3 * cout), f32),
            pltpu.VMEM((2 * group * part, LANES), f32),
            pltpu.VMEM((2, group, part, LANES), f32),
            pltpu.VMEM((group, part, LANES), f32),
            pltpu.VMEM((group, part, LANES), f32),
            pltpu.VMEM((group, part, LANES), f32),
            pltpu.VMEM((nz, part, LANES), f32),
            pltpu.VMEM((2, group, part, LANES), f32),
            pltpu.VMEM((ni, cout, nj, nk), bf16),
            pltpu.VMEM((ni, cin, nj, nk), bf16),
            dma((3,)),
            dma((2 * ni,)),
            dma((8,)), dma((8,)), dma((8,)), dma((8,)),
            dma((1,)), dma((1,)),
            dma((group,)), dma((group,)),
            dma((nz,)), dma((nz,)),
            dma((group,)), dma((group,)),
            dma((group,)), dma((group,)),
        ],
        compiler_params=pltpu.CompilerParams(
            collective_id=0, has_side_effects=True, vmem_limit_bytes=48 * 1024 * 1024
        ),
        cost_estimate=pl.CostEstimate(flops=3_000_000_000, bytes_accessed=4_000_000, transcendentals=0),
    )(*(pltpu.with_memory_space_constraint(x, pltpu.HBM) for x in (activations[0], taps, out_grad[0])))
    kernel_grad = kernel_grad.reshape(3, 3, 3, cin, cout).transpose(4, 3, 0, 1, 2)
    return (output[None], in_grad[None], kernel_grad)


def solution(mesh):
    sizes = (mesh.shape["dp"], mesh.shape["gx"], mesh.shape["gy"])
    return jax.shard_map(
        functools.partial(local, sizes),
        mesh=mesh,
        in_specs=(P("dp", None, "gx", "gy", None), P(), P("dp", None, "gx", "gy", None)),
        out_specs=(P("dp", None, "gx", "gy", None), P("dp", None, "gx", "gy", None), P()),
        check_vma=False,
    )
```

```python
import functools
import math

import jax
import jax.numpy as jnp
from jax import lax
from jax.experimental import pallas as pl
from jax.experimental.pallas import tpu as pltpu
from jax.sharding import PartitionSpec as P

MESH = pl.DeviceIdType.MESH
LANES = 128
AROUND = [(-1, 0), (1, 0), (0, -1), (0, 1), (-1, -1), (-1, 1), (1, -1), (1, 1)]


def kernel(sizes, scale, act_hbm, w_hbm, og_hbm, out_hbm, ing_hbm, kg_ref,
           act_v, w_v, og_v, act_e, og_e, og_r, land_x, land_y, land_c, stage, w_fwd, w_bwd, grad, dense, slots, near, sums, parts, lifted, full,
           out_v, ing_v, in_sem, out_sem, ha_send, ha_recv, ho_send, ho_recv,
           p1_send, p1_recv, p2_send, p2_recv, p3_send, p3_recv, p4_send, p4_recv, p5_send, p5_recv):
    n_dp, n_gx, n_gy = sizes
    cin, ni, nj, _ = act_v.shape
    cout = og_v.shape[0]
    nz = n_gx // 2
    group = n_dp * n_gy
    dp, gx, gy = lax.axis_index("dp"), lax.axis_index("gx"), lax.axis_index("gy")
    z, core = lax.div(gx, 2), lax.rem(gx, 2)
    place = dp * n_gy + gy

    def shifted(di, dj):
        return (dp, lax.rem(gx + di + n_gx, n_gx), lax.rem(gy + dj + n_gy, n_gy))

    def along_z(dz):
        return (dp, lax.rem(z + dz, nz) * 2 + core, gy)

    other_core = (dp, z * 2 + 1 - core, gy)

    def across(d):
        return (lax.rem(dp + lax.div(d, n_gy), n_dp), gx, lax.rem(gy + lax.rem(d, n_gy), n_gy))

    def place_across(d):
        return lax.rem(dp + lax.div(d, n_gy), n_dp) * n_gy + lax.rem(gy + lax.rem(d, n_gy), n_gy)

    def source_across(d):
        return lax.rem(dp - lax.div(d, n_gy) + n_dp, n_dp) * n_gy + lax.rem(gy - lax.rem(d, n_gy) + n_gy, n_gy)

    barrier = pltpu.get_barrier_semaphore()

    def greet(target):
        pl.semaphore_signal(barrier, inc=1, device_id=target, device_id_type=MESH)

    for di, dj in AROUND:
        greet(shifted(di, dj))
    lax.fori_loop(2, n_gy - 1, lambda d, c: (greet(across(d)), c)[1], 0)
    lax.fori_loop(n_gy, group, lambda d, c: (greet(across(d)), c)[1], 0)
    lax.fori_loop(1, nz, lambda d, c: (greet(along_z(d)), c)[1], 0)

    act_in = pltpu.make_async_copy(act_hbm, act_v, in_sem.at[0])
    og_in = pltpu.make_async_copy(og_hbm, og_v, in_sem.at[1])
    w_in = pltpu.make_async_copy(w_hbm, w_v, in_sem.at[2])
    act_in.start()
    og_in.start()
    w_in.start()

    def halo(field, n, send, recv, landing=None):
        di, dj = AROUND[n]
        rows = {-1: (1, ni + 1, 1), 0: (1, 1, ni), 1: (ni, 0, 1)}[di]
        cols = {-1: (1, nj + 1, 1), 0: (1, 1, nj), 1: (nj, 0, 1)}[dj]
        if landing is None:
            landing = field.at[pl.ds(rows[1], rows[2]), :, pl.ds(cols[1] * LANES, cols[2] * LANES)]
        return pltpu.make_async_remote_copy(
            src_ref=field.at[pl.ds(rows[0], rows[2]), :, pl.ds(cols[0] * LANES, cols[2] * LANES)],
            dst_ref=landing,
            send_sem=send.at[n],
            recv_sem=recv.at[n],
            device_id=shifted(di, dj),
            device_id_type=MESH,
        )

    def act_halo(n):
        if n < 2:
            landing = land_x.at[pl.ds(n, 1)]
        elif n < 4:
            landing = land_y.at[n - 2]
        else:
            landing = land_c.at[pl.ds(n - 4, 1)]
        return halo(act_e, n, ha_send, ha_recv, landing)

    act_e[0] = jnp.zeros_like(act_e[0])
    act_e[ni + 1] = jnp.zeros_like(act_e[0])
    for edge in (0, nj + 1):
        act_e[pl.ds(1, ni), :, pl.ds(edge * LANES, LANES)] = jnp.zeros((ni, cin, LANES), jnp.bfloat16)
    act_in.wait()

    def turn_act(i, carry):
        stage[pl.ds(0, cin * nj)] = act_v[:, i].astype(jnp.float32).reshape(cin * nj, LANES)
        for j in range(nj):
            act_e[i + 1, :, pl.ds((j + 1) * LANES, LANES)] = stage[pl.ds(j, cin, stride=nj)].astype(jnp.bfloat16)
        return carry

    lax.fori_loop(0, ni, turn_act, 0)
    pl.semaphore_wait(barrier, 6 + (nz - 1) + (group - 1))
    for n in (2, 3, 0, 1, 4, 5, 6, 7):
        act_halo(n).start()

    og_in.wait()

    def turn_og(i, carry):
        stage[...] = og_v[:, i].astype(jnp.float32).reshape(cout * nj, LANES)
        for j in range(nj):
            rows = stage[pl.ds(j, cout, stride=nj)]
            at = pl.ds(j * LANES, LANES)
            og_e[i + 1, :, pl.ds((j + 1) * LANES, LANES)] = rows.astype(jnp.bfloat16)
            og_r[i, pl.ds(0, cout), at] = pltpu.roll(rows, LANES - 1, 1).astype(jnp.bfloat16)
            og_r[i, pl.ds(cout, cout), at] = rows.astype(jnp.bfloat16)
            og_r[i, pl.ds(2 * cout, cout), at] = pltpu.roll(rows, 1, 1).astype(jnp.bfloat16)
        return carry

    lax.fori_loop(0, ni, turn_og, 0)

    def product(taps, cells):
        return lax.dot_general(taps, cells, (((1,), (1,)), ((), ())), preferred_element_type=jnp.float32)

    def weight_term(i):
        taps = jnp.concatenate(
            [act_e[i + a, :, pl.ds(b * LANES, nj * LANES)] for a in range(3) for b in range(3)], axis=0
        )
        return product(taps, og_r[i])

    grad[...] = weight_term(0)
    for i in range(1, ni):
        grad[...] += weight_term(i)

    for n in range(2):
        act_halo(n).wait_recv()
    act_e[ni + 1, :, pl.ds(LANES, nj * LANES)] = land_x[0]
    act_e[0, :, pl.ds(LANES, nj * LANES)] = land_x[1]
    for a, outer, inner in ((0, 0, 0), (2, ni + 1, ni - 1)):
        taps = jnp.concatenate([act_e[outer, :, pl.ds(b * LANES, nj * LANES)] for b in range(3)], axis=0)
        grad[pl.ds(a * 3 * cin, 3 * cin)] += product(taps, og_r[inner])
    for n in range(2, 4):
        act_halo(n).wait_recv()
    act_e[pl.ds(1, ni), :, pl.ds((nj + 1) * LANES, LANES)] = land_y[0]
    act_e[pl.ds(1, ni), :, pl.ds(0, LANES)] = land_y[1]
    for n in range(4, 8):
        act_halo(n).wait_recv()
        di, dj = AROUND[n]
        act_e[ni + 1 if di < 0 else 0, :, pl.ds((nj + 1 if dj < 0 else 0) * LANES, LANES)] = land_c[n - 4]
    for b, outer, inner in ((0, 0, 0), (2, nj + 1, nj - 1)):
        taps = jnp.concatenate(
            [
                jnp.concatenate([act_e[i + a, :, pl.ds(outer * LANES, LANES)] for i in range(ni)], axis=1)
                for a in range(3)
            ],
            axis=0,
        )
        cells = jnp.concatenate([og_r[i, :, pl.ds(inner * LANES, LANES)] for i in range(ni)], axis=1)
        term = product(taps, cells)
        for a in range(3):
            grad[pl.ds((3 * a + b) * cin, cin)] += term[a * cin : (a + 1) * cin]
    tall = 9 * cin
    half = tall // 2
    dense[pl.ds(0, tall)] = grad[:, :LANES]
    dense[pl.ds(tall, half)] = jnp.concatenate([grad[:half, LANES:], grad[half:, LANES:]], axis=1)
    part = slots.shape[2]
    extra = 2 * group * part - tall - half
    if extra:
        dense[pl.ds(tall + half, extra)] = jnp.zeros((extra, LANES), jnp.float32)
    for s in range(2 * group):
        slots[s // group, s % group] = dense[pl.ds(s * part, part)]

    def forward(i):
        for p in range(nj // 2):
            taps = jnp.concatenate(
                [
                    act_e[i + a, :, pl.ds((2 * p + b) * LANES, 2 * LANES)]
                    for a in range(3)
                    for b in range(3)
                ],
                axis=0,
            )
            y = jnp.dot(w_fwd[...], taps, preferred_element_type=jnp.float32)
            for q in range(2):
                t = y[:, q * LANES : (q + 1) * LANES]
                total = t[cout : 2 * cout] + pltpu.roll(t[:cout], 1, 1) + pltpu.roll(t[2 * cout :], LANES - 1, 1)
                stage[pl.ds(2 * p + q, cout, stride=nj)] = total
        out_v[i] = stage[...].astype(jnp.bfloat16).reshape(cout, nj, LANES)
        pltpu.make_async_copy(out_v.at[i], out_hbm.at[:, i], out_sem.at[i]).start()

    def backward(i):
        for p in range(nj // 2):
            taps = jnp.concatenate(
                [
                    og_e[i + 2 - a, :, pl.ds((2 * p + 2 - b) * LANES, 2 * LANES)]
                    for a in range(3)
                    for b in range(3)
                ],
                axis=0,
            )
            y = jnp.dot(w_bwd[...], taps, preferred_element_type=jnp.float32)
            for q in range(2):
                t = y[:, q * LANES : (q + 1) * LANES]
                total = t[cin : 2 * cin] + pltpu.roll(t[:cin], LANES - 1, 1) + pltpu.roll(t[2 * cin :], 1, 1)
                stage[pl.ds(2 * p + q, cin, stride=nj)] = total
        ing_v[i] = stage[pl.ds(0, cin * nj)].astype(jnp.bfloat16).reshape(cin, nj, LANES)
        pltpu.make_async_copy(ing_v.at[i], ing_hbm.at[:, i], out_sem.at[ni + i]).start()

    def to_core():
        return pltpu.make_async_remote_copy(
            src_ref=slots.at[1 - core], dst_ref=near, send_sem=p1_send.at[0], recv_sem=p1_recv.at[0],
            device_id=other_core, device_id_type=MESH)

    def to_group(d):
        return pltpu.make_async_remote_copy(
            src_ref=sums.at[place_across(d)], dst_ref=parts.at[place],
            send_sem=p2_send.at[d], recv_sem=p2_recv.at[d], device_id=across(d), device_id_type=MESH)

    def to_z(dz):
        return pltpu.make_async_remote_copy(
            src_ref=lifted.at[z], dst_ref=lifted.at[z], send_sem=p3_send.at[dz], recv_sem=p3_recv.at[dz],
            device_id=along_z(dz), device_id_type=MESH)

    def back_group(d):
        return pltpu.make_async_remote_copy(
            src_ref=full.at[core, place], dst_ref=full.at[core, place], send_sem=p4_send.at[d], recv_sem=p4_recv.at[d],
            device_id=across(d), device_id_type=MESH)

    def back_core(d):
        at = source_across(d)
        return pltpu.make_async_remote_copy(
            src_ref=full.at[core, at], dst_ref=full.at[core, at], send_sem=p5_send.at[d], recv_sem=p5_recv.at[d],
            device_id=other_core, device_id_type=MESH)

    def each(low, high, do):
        def body(t, carry):
            do(t)
            return carry

        lax.fori_loop(low, high, body, 0)

    to_core().start()
    w_in.wait()
    w = w_v[...].astype(jnp.float32).reshape(9, 3, cin, cout)
    by_tap = jnp.concatenate([w[:, e].reshape(9 * cin, cout) for e in range(3)], axis=1)
    w_fwd[...] = by_tap.T.astype(jnp.bfloat16)
    w_bwd[...] = jnp.concatenate([w[n].reshape(3 * cin, cout) for n in range(9)], axis=1).astype(jnp.bfloat16)
    to_core().wait_recv()
    sums[...] = slots[core] + near[...]
    each(1, group, lambda d: to_group(group - d).start())
    for n in range(2):
        halo(og_e, n, ho_send, ho_recv).start()
    parts[place] = sums[place]
    each(0, 2, forward)
    each(1, group, lambda d: to_group(d).wait_recv())
    lifted[z] = jnp.sum(parts[...], axis=0)
    each(1, nz, lambda dz: to_z(dz).start())
    for n in range(2, 8):
        halo(og_e, n, ho_send, ho_recv).start()
    each(2, ni, forward)
    each(1, nz, lambda dz: to_z(dz).wait_recv())
    full[core, place] = jnp.sum(lifted[...], axis=0) * jnp.float32(scale)
    each(1, group, lambda d: back_group(d).start())
    back_core(0).start()
    for n in range(8):
        halo(og_e, n, ho_send, ho_recv).wait_recv()
    each(0, ni, backward)

    def forward_core(t):
        d = t + 1
        back_group(d).wait_recv()
        back_core(d).start()

    each(0, group - 1, forward_core)
    each(0, group, lambda d: back_core(d).wait_recv())
    for s in range(2 * group):
        dense[pl.ds(s * part, part)] = full[s // group, s % group]
    for n in range(9):
        rows = pl.ds(n * cin, cin)
        kg_ref[pl.ds(n * 3 * cin, cin)] = dense[rows, pl.ds(0, cout)]
        kg_ref[pl.ds((n * 3 + 1) * cin, cin)] = dense[rows, pl.ds(cout, cout)]
    third = jnp.concatenate([dense[pl.ds(tall, half), :cout], dense[pl.ds(tall, half), cout:]], axis=0)
    for n in range(9):
        kg_ref[pl.ds((n * 3 + 2) * cin, cin)] = third[n * cin : (n + 1) * cin]

    for n in range(8):
        act_halo(n).wait_send()
        halo(og_e, n, ho_send, ho_recv).wait_send()
    to_core().wait_send()
    each(1, group, lambda d: to_group(d).wait_send())
    each(1, nz, lambda dz: to_z(dz).wait_send())
    each(1, group, lambda d: back_group(d).wait_send())
    each(0, group, lambda d: back_core(d).wait_send())
    each(0, ni, lambda i: pltpu.make_async_copy(out_v.at[i], out_hbm.at[:, i], out_sem.at[i]).wait())
    each(0, ni, lambda i: pltpu.make_async_copy(ing_v.at[i], ing_hbm.at[:, i], out_sem.at[ni + i]).wait())


def deliver(*refs):
    count = len(refs) // 2
    sem = refs[-1]
    copies = [pltpu.make_async_copy(refs[n], refs[count + n], sem.at[n]) for n in range(count)]
    for copy in copies:
        copy.start()
    for copy in copies:
        copy.wait()


def local(sizes, activations, weights, out_grad):
    n_dp, n_gx, n_gy = sizes
    univ, cin, ni, nj, nk = activations.shape
    cout = out_grad.shape[1]
    nz, group = n_gx // 2, n_dp * n_gy
    scale = 1.0 / math.sqrt(univ * n_dp * ni * n_gx * nj * n_gy * nk)
    part = -(-27 * cin * cout // (LANES * 2 * group))
    bf16, f32 = jnp.bfloat16, jnp.float32
    dma = pltpu.SemaphoreType.DMA
    taps = weights.transpose(2, 3, 4, 1, 0).reshape(27 * cin, cout)
    output, in_grad, kernel_grad = pl.pallas_call(
        functools.partial(kernel, sizes, scale),
        out_shape=(
            jax.ShapeDtypeStruct((cout, ni, nj, nk), bf16),
            jax.ShapeDtypeStruct((cin, ni, nj, nk), bf16),
            jax.ShapeDtypeStruct((27 * cin, cout), f32),
        ),
        in_specs=[
            pl.BlockSpec(memory_space=pltpu.HBM),
            pl.BlockSpec(memory_space=pltpu.HBM),
            pl.BlockSpec(memory_space=pltpu.HBM),
        ],
        out_specs=(
            pl.BlockSpec(memory_space=pl.ANY),
            pl.BlockSpec(memory_space=pl.ANY),
            pl.BlockSpec(memory_space=pltpu.VMEM),
        ),
        scratch_shapes=[
            pltpu.VMEM((cin, ni, nj, nk), bf16),
            pltpu.VMEM((27 * cin, cout), bf16),
            pltpu.VMEM((cout, ni, nj, nk), bf16),
            pltpu.VMEM((ni + 2, cin, (nj + 2) * nk), bf16),
            pltpu.VMEM((ni + 2, cout, (nj + 2) * nk), bf16),
            pltpu.VMEM((ni, 3 * cout, nj * nk), bf16),
            pltpu.VMEM((2, cin, nj * nk), bf16),
            pltpu.VMEM((2, ni, cin, nk), bf16),
            pltpu.VMEM((4, cin, nk), bf16),
            pltpu.VMEM((cout * nj, nk), f32),
            pltpu.VMEM((3 * cout, 9 * cin), bf16),
            pltpu.VMEM((3 * cin, 9 * cout), bf16),
            pltpu.VMEM((9 * cin, 3 * cout), f32),
            pltpu.VMEM((2 * group * part, LANES), f32),
            pltpu.VMEM((2, group, part, LANES), f32),
            pltpu.VMEM((group, part, LANES), f32),
            pltpu.VMEM((group, part, LANES), f32),
            pltpu.VMEM((group, part, LANES), f32),
            pltpu.VMEM((nz, part, LANES), f32),
            pltpu.VMEM((2, group, part, LANES), f32),
            pltpu.VMEM((ni, cout, nj, nk), bf16),
            pltpu.VMEM((ni, cin, nj, nk), bf16),
            dma((3,)),
            dma((2 * ni,)),
            dma((8,)), dma((8,)), dma((8,)), dma((8,)),
            dma((1,)), dma((1,)),
            dma((group,)), dma((group,)),
            dma((nz,)), dma((nz,)),
            dma((group,)), dma((group,)),
            dma((group,)), dma((group,)),
        ],
        compiler_params=pltpu.CompilerParams(
            collective_id=0, has_side_effects=True, vmem_limit_bytes=48 * 1024 * 1024
        ),
        cost_estimate=pl.CostEstimate(flops=3_000_000_000, bytes_accessed=4_000_000, transcendentals=0),
    )(*(pltpu.with_memory_space_constraint(x, pltpu.HBM) for x in (activations[0], taps, out_grad[0])))
    held = tuple(pltpu.with_memory_space_constraint(x, pltpu.VMEM) for x in (output, in_grad, kernel_grad))
    output, in_grad, kernel_grad = pl.pallas_call(
        deliver,
        out_shape=tuple(jax.ShapeDtypeStruct(x.shape, x.dtype) for x in held),
        in_specs=[pl.BlockSpec(memory_space=pltpu.VMEM)] * 3,
        out_specs=(pl.BlockSpec(memory_space=pltpu.HBM),) * 3,
        scratch_shapes=[dma((3,))],
    )(*held)
    kernel_grad = kernel_grad.reshape(3, 3, 3, cin, cout).transpose(4, 3, 0, 1, 2)
    return (output[None], in_grad[None], kernel_grad)


def solution(mesh):
    sizes = (mesh.shape["dp"], mesh.shape["gx"], mesh.shape["gy"])
    return jax.shard_map(
        functools.partial(local, sizes),
        mesh=mesh,
        in_specs=(P("dp", None, "gx", "gy", None), P(), P("dp", None, "gx", "gy", None)),
        out_specs=(P("dp", None, "gx", "gy", None), P("dp", None, "gx", "gy", None), P()),
        check_vma=False,
    )
```

```python
import functools
import math

import jax
import jax.numpy as jnp
from jax import lax
from jax.experimental import pallas as pl
from jax.experimental.pallas import tpu as pltpu
from jax.sharding import PartitionSpec as P

MESH = pl.DeviceIdType.MESH
LANES = 128
AROUND = [(-1, 0), (1, 0), (0, -1), (0, 1), (-1, -1), (-1, 1), (1, -1), (1, 1)]


def kernel(sizes, scale, act_hbm, w_hbm, og_hbm, out_hbm, ing_hbm, full,
           act_v, w_v, og_v, act_e, og_e, og_r, land_x, land_y, land_c, stage, w_fwd, w_bwd, grad, dense, slots, parts, lifted, mine,
           out_v, ing_v, in_sem, out_sem, ha_send, ha_recv, ho_send, ho_recv,
           p1_send, p1_recv, p2_send, p2_recv, p3_send, p3_recv, mine_sem):
    n_dp, n_gx, n_gy = sizes
    cin, ni, nj, _ = act_v.shape
    cout = og_v.shape[0]
    nz = n_gx // 2
    group = n_dp * n_gy
    dp, gx, gy = lax.axis_index("dp"), lax.axis_index("gx"), lax.axis_index("gy")
    z, core = lax.div(gx, 2), lax.rem(gx, 2)
    place = dp * n_gy + gy

    def shifted(di, dj):
        return (dp, lax.rem(gx + di + n_gx, n_gx), lax.rem(gy + dj + n_gy, n_gy))

    def along_z(dz):
        return (dp, lax.rem(z + dz, nz) * 2 + core, gy)

    def across(d, flip=0):
        return (
            lax.rem(dp + lax.div(d, n_gy), n_dp),
            z * 2 + core + flip * (1 - 2 * core),
            lax.rem(gy + lax.rem(d, n_gy), n_gy),
        )

    def place_across(d):
        return lax.rem(dp + lax.div(d, n_gy), n_dp) * n_gy + lax.rem(gy + lax.rem(d, n_gy), n_gy)

    act_in = pltpu.make_async_copy(act_hbm, act_v, in_sem.at[0])
    og_in = pltpu.make_async_copy(og_hbm, og_v, in_sem.at[1])
    w_in = pltpu.make_async_copy(w_hbm, w_v, in_sem.at[2])
    act_in.start()
    og_in.start()
    w_in.start()

    barrier = pltpu.get_barrier_semaphore()

    def greet(target):
        pl.semaphore_signal(barrier, inc=1, device_id=target, device_id_type=MESH)

    steps = [(d, flip) for d in range(2, group) for flip in range(2) if d not in (n_gy - 1,)]
    hops = {}
    for d, flip in steps:
        far_x, far_y = 2 * (d // n_gy), d % n_gy
        hops[d, flip] = min(far_y, n_gy - far_y) / 2 + (1.5 if far_y % 2 else far_x)
    targets = [(hops[d, flip], across(d, flip)) for d, flip in steps]
    targets += [(min(d, nz - d), along_z(d)) for d in range(1, nz)]
    targets += [(abs(di) + 1.5 * abs(dj), shifted(di, dj)) for di, dj in AROUND]
    for _, target in sorted(targets, key=lambda t: -t[0]):
        greet(target)

    def halo(field, n, send, recv, landing=None):
        di, dj = AROUND[n]
        rows = {-1: (1, ni + 1, 1), 0: (1, 1, ni), 1: (ni, 0, 1)}[di]
        cols = {-1: (1, nj + 1, 1), 0: (1, 1, nj), 1: (nj, 0, 1)}[dj]
        if landing is None:
            landing = field.at[pl.ds(rows[1], rows[2]), :, pl.ds(cols[1] * LANES, cols[2] * LANES)]
        return pltpu.make_async_remote_copy(
            src_ref=field.at[pl.ds(rows[0], rows[2]), :, pl.ds(cols[0] * LANES, cols[2] * LANES)],
            dst_ref=landing,
            send_sem=send.at[n],
            recv_sem=recv.at[n],
            device_id=shifted(di, dj),
            device_id_type=MESH,
        )

    def act_halo(n):
        if n < 2:
            landing = land_x.at[pl.ds(n, 1)]
        elif n < 4:
            landing = land_y.at[n - 2]
        else:
            landing = land_c.at[pl.ds(n - 4, 1)]
        return halo(act_e, n, ha_send, ha_recv, landing)

    act_e[0] = jnp.zeros_like(act_e[0])
    act_e[ni + 1] = jnp.zeros_like(act_e[0])
    for edge in (0, nj + 1):
        act_e[pl.ds(1, ni), :, pl.ds(edge * LANES, LANES)] = jnp.zeros((ni, cin, LANES), jnp.bfloat16)
    act_in.wait()

    def turn_act(i, carry):
        stage[pl.ds(0, cin * nj)] = act_v[:, i].astype(jnp.float32).reshape(cin * nj, LANES)
        for j in range(nj):
            act_e[i + 1, :, pl.ds((j + 1) * LANES, LANES)] = stage[pl.ds(j, cin, stride=nj)].astype(jnp.bfloat16)
        return carry

    lax.fori_loop(0, ni, turn_act, 0)
    pl.semaphore_wait(barrier, 8 + 2 * (group - 3) + (nz - 1))
    for n in (2, 3, 0, 1, 4, 5, 6, 7):
        act_halo(n).start()

    og_in.wait()

    def turn_og(i, carry):
        stage[...] = og_v[:, i].astype(jnp.float32).reshape(cout * nj, LANES)
        for j in range(nj):
            rows = stage[pl.ds(j, cout, stride=nj)]
            at = pl.ds(j * LANES, LANES)
            og_e[i + 1, :, pl.ds((j + 1) * LANES, LANES)] = rows.astype(jnp.bfloat16)
            og_r[i, pl.ds(0, cout), at] = pltpu.roll(rows, LANES - 1, 1).astype(jnp.bfloat16)
            og_r[i, pl.ds(cout, cout), at] = rows.astype(jnp.bfloat16)
            og_r[i, pl.ds(2 * cout, cout), at] = pltpu.roll(rows, 1, 1).astype(jnp.bfloat16)
        return carry

    lax.fori_loop(0, ni, turn_og, 0)

    def product(taps, cells):
        return lax.dot_general(taps, cells, (((1,), (1,)), ((), ())), preferred_element_type=jnp.float32)

    def weight_term(i):
        taps = jnp.concatenate(
            [act_e[i + a, :, pl.ds(b * LANES, nj * LANES)] for a in range(3) for b in range(3)], axis=0
        )
        return product(taps, og_r[i])

    grad[...] = weight_term(0)
    for i in range(1, ni):
        grad[...] += weight_term(i)

    for n in range(2):
        act_halo(n).wait_recv()
    act_e[ni + 1, :, pl.ds(LANES, nj * LANES)] = land_x[0]
    act_e[0, :, pl.ds(LANES, nj * LANES)] = land_x[1]
    for a, outer, inner in ((0, 0, 0), (2, ni + 1, ni - 1)):
        taps = jnp.concatenate([act_e[outer, :, pl.ds(b * LANES, nj * LANES)] for b in range(3)], axis=0)
        grad[pl.ds(a * 3 * cin, 3 * cin)] += product(taps, og_r[inner])
    for n in range(2, 4):
        act_halo(n).wait_recv()
    act_e[pl.ds(1, ni), :, pl.ds((nj + 1) * LANES, LANES)] = land_y[0]
    act_e[pl.ds(1, ni), :, pl.ds(0, LANES)] = land_y[1]
    for n in range(4, 8):
        act_halo(n).wait_recv()
        di, dj = AROUND[n]
        act_e[ni + 1 if di < 0 else 0, :, pl.ds((nj + 1 if dj < 0 else 0) * LANES, LANES)] = land_c[n - 4]
    for b, outer, inner in ((0, 0, 0), (2, nj + 1, nj - 1)):
        taps = jnp.concatenate(
            [
                jnp.concatenate([act_e[i + a, :, pl.ds(outer * LANES, LANES)] for i in range(ni)], axis=1)
                for a in range(3)
            ],
            axis=0,
        )
        cells = jnp.concatenate([og_r[i, :, pl.ds(inner * LANES, LANES)] for i in range(ni)], axis=1)
        term = product(taps, cells)
        for a in range(3):
            grad[pl.ds((3 * a + b) * cin, cin)] += term[a * cin : (a + 1) * cin]
    tall = 9 * cin
    half = tall // 2
    dense[pl.ds(0, tall)] = grad[:, :LANES]
    dense[pl.ds(tall, half)] = jnp.concatenate([grad[:half, LANES:], grad[half:, LANES:]], axis=1)
    part = slots.shape[2]
    extra = 2 * group * part - tall - half
    if extra:
        dense[pl.ds(tall + half, extra)] = jnp.zeros((extra, LANES), jnp.float32)
    for s in range(2 * group):
        slots[s // group, s % group] = dense[pl.ds(s * part, part)]

    def forward(i):
        for p in range(nj // 2):
            taps = jnp.concatenate(
                [
                    act_e[i + a, :, pl.ds((2 * p + b) * LANES, 2 * LANES)]
                    for a in range(3)
                    for b in range(3)
                ],
                axis=0,
            )
            y = jnp.dot(w_fwd[...], taps, preferred_element_type=jnp.float32)
            for q in range(2):
                t = y[:, q * LANES : (q + 1) * LANES]
                total = t[cout : 2 * cout] + pltpu.roll(t[:cout], 1, 1) + pltpu.roll(t[2 * cout :], LANES - 1, 1)
                stage[pl.ds(2 * p + q, cout, stride=nj)] = total
        out_v[i] = stage[...].astype(jnp.bfloat16).reshape(cout, nj, LANES)
        pltpu.make_async_copy(out_v.at[i], out_hbm.at[:, i], out_sem.at[i]).start()

    def backward(i):
        for p in range(nj // 2):
            taps = jnp.concatenate(
                [
                    og_e[i + 2 - a, :, pl.ds((2 * p + 2 - b) * LANES, 2 * LANES)]
                    for a in range(3)
                    for b in range(3)
                ],
                axis=0,
            )
            y = jnp.dot(w_bwd[...], taps, preferred_element_type=jnp.float32)
            for q in range(2):
                t = y[:, q * LANES : (q + 1) * LANES]
                total = t[cin : 2 * cin] + pltpu.roll(t[:cin], LANES - 1, 1) + pltpu.roll(t[2 * cin :], 1, 1)
                stage[pl.ds(2 * p + q, cin, stride=nj)] = total
        ing_v[i] = stage[pl.ds(0, cin * nj)].astype(jnp.bfloat16).reshape(cin, nj, LANES)
        pltpu.make_async_copy(ing_v.at[i], ing_hbm.at[:, i], out_sem.at[ni + i]).start()

    def to_group(q):
        d, flip = lax.div(q, 2), lax.rem(q, 2)
        return pltpu.make_async_remote_copy(
            src_ref=slots.at[core + flip * (1 - 2 * core), place_across(d)], dst_ref=parts.at[core, place],
            send_sem=p1_send.at[q], recv_sem=p1_recv.at[q], device_id=across(d, flip), device_id_type=MESH)

    def to_z(dz):
        return pltpu.make_async_remote_copy(
            src_ref=lifted.at[z], dst_ref=lifted.at[z], send_sem=p2_send.at[dz], recv_sem=p2_recv.at[dz],
            device_id=along_z(dz), device_id_type=MESH)

    def back_group(q):
        return pltpu.make_async_remote_copy(
            src_ref=mine, dst_ref=full.at[core, place], send_sem=p3_send.at[q], recv_sem=p3_recv.at[q],
            device_id=across(lax.div(q, 2), lax.rem(q, 2)), device_id_type=MESH)

    own = pltpu.make_async_copy(mine, full.at[core, place], mine_sem.at[0])

    def each(low, high, do):
        def body(t, carry):
            do(t)
            return carry

        lax.fori_loop(low, high, body, 0)

    peers = 2 * group
    each(1, peers, lambda t: to_group(peers - t).start())
    parts[core, place] = slots[core, place]
    for n in range(2):
        halo(og_e, n, ho_send, ho_recv).start()
    w_in.wait()
    w = w_v[...].astype(jnp.float32).reshape(9, 3, cin, cout)
    by_tap = jnp.concatenate([w[:, e].reshape(9 * cin, cout) for e in range(3)], axis=1)
    w_fwd[...] = by_tap.T.astype(jnp.bfloat16)
    w_bwd[...] = jnp.concatenate([w[n].reshape(3 * cin, cout) for n in range(9)], axis=1).astype(jnp.bfloat16)
    each(0, 2, forward)
    each(1, peers, lambda q: to_group(q).wait_recv())
    lifted[z] = jnp.sum(parts[...], axis=(0, 1))
    each(1, nz, lambda dz: to_z(dz).start())
    for n in range(2, 8):
        halo(og_e, n, ho_send, ho_recv).start()
    each(2, ni, forward)
    each(1, nz, lambda dz: to_z(dz).wait_recv())
    mine[...] = jnp.sum(lifted[...], axis=0) * jnp.float32(scale)
    each(1, peers, lambda t: back_group(peers - t).start())
    own.start()
    for n in range(8):
        halo(og_e, n, ho_send, ho_recv).wait_recv()
    each(0, ni, backward)


    for n in range(8):
        act_halo(n).wait_send()
        halo(og_e, n, ho_send, ho_recv).wait_send()
    each(1, peers, lambda q: to_group(q).wait_send())
    each(1, nz, lambda dz: to_z(dz).wait_send())
    each(1, peers, lambda q: back_group(q).wait_send())
    each(0, ni, lambda i: pltpu.make_async_copy(out_v.at[i], out_hbm.at[:, i], out_sem.at[i]).wait())
    each(0, ni, lambda i: pltpu.make_async_copy(ing_v.at[i], ing_hbm.at[:, i], out_sem.at[ni + i]).wait())
    own.wait()
    each(1, peers, lambda q: back_group(q).wait_recv())


def deliver(cin, cout, out_v, ing_v, full, out_hbm, ing_hbm, kg_hbm, dense, kg_v, sem):
    copies = [
        pltpu.make_async_copy(source, target, sem.at[n])
        for n, (source, target) in enumerate(((out_v, out_hbm), (ing_v, ing_hbm), (kg_v, kg_hbm)))
    ]
    copies[0].start()
    copies[1].start()
    _, group, part, _ = full.shape
    tall = 9 * cin
    half = tall // 2
    for s in range(2 * group):
        dense[pl.ds(s * part, part)] = full[s // group, s % group]
    for n in range(9):
        rows = pl.ds(n * cin, cin)
        kg_v[pl.ds(n * 3 * cin, cin)] = dense[rows, pl.ds(0, cout)]
        kg_v[pl.ds((n * 3 + 1) * cin, cin)] = dense[rows, pl.ds(cout, cout)]
    third = jnp.concatenate([dense[pl.ds(tall, half), :cout], dense[pl.ds(tall, half), cout:]], axis=0)
    for n in range(9):
        kg_v[pl.ds((n * 3 + 2) * cin, cin)] = third[n * cin : (n + 1) * cin]
    copies[2].start()
    for copy in copies:
        copy.wait()


def local(sizes, activations, weights, out_grad):
    n_dp, n_gx, n_gy = sizes
    univ, cin, ni, nj, nk = activations.shape
    cout = out_grad.shape[1]
    nz, group = n_gx // 2, n_dp * n_gy
    scale = 1.0 / math.sqrt(univ * n_dp * ni * n_gx * nj * n_gy * nk)
    part = -(-27 * cin * cout // (LANES * 2 * group))
    bf16, f32 = jnp.bfloat16, jnp.float32
    dma = pltpu.SemaphoreType.DMA
    taps = weights.transpose(2, 3, 4, 1, 0).reshape(27 * cin, cout)
    output, in_grad, gathered = pl.pallas_call(
        functools.partial(kernel, sizes, scale),
        out_shape=(
            jax.ShapeDtypeStruct((cout, ni, nj, nk), bf16),
            jax.ShapeDtypeStruct((cin, ni, nj, nk), bf16),
            jax.ShapeDtypeStruct((2, group, part, LANES), f32),
        ),
        in_specs=[
            pl.BlockSpec(memory_space=pltpu.HBM),
            pl.BlockSpec(memory_space=pltpu.HBM),
            pl.BlockSpec(memory_space=pltpu.HBM),
        ],
        out_specs=(
            pl.BlockSpec(memory_space=pl.ANY),
            pl.BlockSpec(memory_space=pl.ANY),
            pl.BlockSpec(memory_space=pl.ANY),
        ),
        scratch_shapes=[
            pltpu.VMEM((cin, ni, nj, nk), bf16),
            pltpu.VMEM((27 * cin, cout), bf16),
            pltpu.VMEM((cout, ni, nj, nk), bf16),
            pltpu.VMEM((ni + 2, cin, (nj + 2) * nk), bf16),
            pltpu.VMEM((ni + 2, cout, (nj + 2) * nk), bf16),
            pltpu.VMEM((ni, 3 * cout, nj * nk), bf16),
            pltpu.VMEM((2, cin, nj * nk), bf16),
            pltpu.VMEM((2, ni, cin, nk), bf16),
            pltpu.VMEM((4, cin, nk), bf16),
            pltpu.VMEM((cout * nj, nk), f32),
            pltpu.VMEM((3 * cout, 9 * cin), bf16),
            pltpu.VMEM((3 * cin, 9 * cout), bf16),
            pltpu.VMEM((9 * cin, 3 * cout), f32),
            pltpu.VMEM((2 * group * part, LANES), f32),
            pltpu.VMEM((2, group, part, LANES), f32),
            pltpu.VMEM((2, group, part, LANES), f32),
            pltpu.VMEM((nz, part, LANES), f32),
            pltpu.VMEM((part, LANES), f32),
            pltpu.VMEM((ni, cout, nj, nk), bf16),
            pltpu.VMEM((ni, cin, nj, nk), bf16),
            dma((3,)),
            dma((2 * ni,)),
            dma((8,)), dma((8,)), dma((8,)), dma((8,)),
            dma((2 * group,)), dma((2 * group,)),
            dma((nz,)), dma((nz,)),
            dma((2 * group,)), dma((2 * group,)),
            dma((1,)),
        ],
        compiler_params=pltpu.CompilerParams(
            collective_id=0, has_side_effects=True, vmem_limit_bytes=48 * 1024 * 1024
        ),
        cost_estimate=pl.CostEstimate(flops=3_000_000_000, bytes_accessed=4_000_000, transcendentals=0),
    )(*(pltpu.with_memory_space_constraint(x, pltpu.HBM) for x in (activations[0], taps, out_grad[0])))
    held = tuple(pltpu.with_memory_space_constraint(x, pltpu.VMEM) for x in (output, in_grad, gathered))
    output, in_grad, kernel_grad = pl.pallas_call(
        functools.partial(deliver, cin, cout),
        out_shape=(
            jax.ShapeDtypeStruct(output.shape, bf16),
            jax.ShapeDtypeStruct(in_grad.shape, bf16),
            jax.ShapeDtypeStruct((27 * cin, cout), f32),
        ),
        in_specs=[pl.BlockSpec(memory_space=pltpu.VMEM)] * 3,
        out_specs=(pl.BlockSpec(memory_space=pltpu.HBM),) * 3,
        scratch_shapes=[
            pltpu.VMEM((2 * group * part, LANES), f32),
            pltpu.VMEM((27 * cin, cout), f32),
            dma((3,)),
        ],
    )(*held)
    kernel_grad = kernel_grad.reshape(3, 3, 3, cin, cout).transpose(4, 3, 0, 1, 2)
    return (output[None], in_grad[None], kernel_grad)


def solution(mesh):
    sizes = (mesh.shape["dp"], mesh.shape["gx"], mesh.shape["gy"])
    return jax.shard_map(
        functools.partial(local, sizes),
        mesh=mesh,
        in_specs=(P("dp", None, "gx", "gy", None), P(), P("dp", None, "gx", "gy", None)),
        out_specs=(P("dp", None, "gx", "gy", None), P("dp", None, "gx", "gy", None), P()),
        check_vma=False,
    )
```

```python
import functools
import math

import jax
import jax.numpy as jnp
from jax import lax
from jax.experimental import pallas as pl
from jax.experimental.pallas import tpu as pltpu
from jax.sharding import PartitionSpec as P

MESH = pl.DeviceIdType.MESH
LANES = 128
AROUND = [(-1, 0), (1, 0), (0, -1), (0, 1), (-1, -1), (-1, 1), (1, -1), (1, 1)]


def kernel(sizes, scale, act_hbm, w_hbm, og_hbm, out_hbm, ing_hbm, full,
           act_v, w_v, og_v, act_e, og_e, og_r, land_x, land_y, land_c, stage, w_fwd, w_bwd, grad, dense, slots, parts, lifted, mine,
           out_v, ing_v, in_sem, out_sem, ha_send, ha_recv, ho_send, ho_recv,
           p1_send, p1_recv, p2_send, p2_recv, p3_send, p3_recv, mine_sem, seen):
    n_dp, n_gx, n_gy = sizes
    cin, ni, nj, _ = act_v.shape
    cout = og_v.shape[0]
    nz = n_gx // 2
    group = n_dp * n_gy
    dp, gx, gy = lax.axis_index("dp"), lax.axis_index("gx"), lax.axis_index("gy")
    z, core = lax.div(gx, 2), lax.rem(gx, 2)
    place = dp * n_gy + gy

    def shifted(di, dj):
        return (dp, lax.rem(gx + di + n_gx, n_gx), lax.rem(gy + dj + n_gy, n_gy))

    def along_z(dz):
        return (dp, lax.rem(z + dz + nz, nz) * 2 + core, gy)

    def across(d, flip=0):
        return (
            lax.rem(dp + d // n_gy, n_dp),
            z * 2 + core + flip * (1 - 2 * core),
            lax.rem(gy + d % n_gy, n_gy),
        )

    def place_across(d):
        return lax.rem(dp + d // n_gy, n_dp) * n_gy + lax.rem(gy + d % n_gy, n_gy)

    act_in = pltpu.make_async_copy(act_hbm, act_v, in_sem.at[0])
    og_in = pltpu.make_async_copy(og_hbm, og_v, in_sem.at[1])
    w_in = pltpu.make_async_copy(w_hbm, w_v, in_sem.at[2])
    act_in.start()
    og_in.start()
    w_in.start()

    barrier = pltpu.get_barrier_semaphore()

    def greet(target):
        pl.semaphore_signal(barrier, inc=1, device_id=target, device_id_type=MESH)

    def hops(d):
        far_y = d % n_gy
        return min(far_y, n_gy - far_y) / 2 + (1.5 if far_y % 2 else 2 * (d // n_gy))

    peers = 2 * group
    far_first = sorted(range(1, peers), key=lambda q: -hops(q // 2))
    near = [(hops(d), across(d, flip)) for d in range(2, group) for flip in range(2) if d != n_gy - 1 and hops(d) <= 2]
    near += [(d, along_z(way * d)) for d in range(1, min(nz, 3)) for way in (1, -1)]
    near += [(abs(di) + 1.5 * abs(dj), shifted(di, dj)) for di, dj in AROUND]
    for _, target in sorted(near, key=lambda t: -t[0]):
        greet(target)

    def tell():
        for target in (across(n_gy % group), across(n_gy // 2), along_z(2), along_z(-2)):
            pl.semaphore_signal(seen, inc=1, device_id=target, device_id_type=MESH)

    def halo(field, n, send, recv, landing=None):
        di, dj = AROUND[n]
        rows = {-1: (1, ni + 1, 1), 0: (1, 1, ni), 1: (ni, 0, 1)}[di]
        cols = {-1: (1, nj + 1, 1), 0: (1, 1, nj), 1: (nj, 0, 1)}[dj]
        if landing is None:
            landing = field.at[pl.ds(rows[1], rows[2]), :, pl.ds(cols[1] * LANES, cols[2] * LANES)]
        return pltpu.make_async_remote_copy(
            src_ref=field.at[pl.ds(rows[0], rows[2]), :, pl.ds(cols[0] * LANES, cols[2] * LANES)],
            dst_ref=landing,
            send_sem=send.at[n],
            recv_sem=recv.at[n],
            device_id=shifted(di, dj),
            device_id_type=MESH,
        )

    def act_halo(n):
        if n < 2:
            landing = land_x.at[pl.ds(n, 1)]
        elif n < 4:
            landing = land_y.at[n - 2]
        else:
            landing = land_c.at[pl.ds(n - 4, 1)]
        return halo(act_e, n, ha_send, ha_recv, landing)

    act_e[0] = jnp.zeros_like(act_e[0])
    act_e[ni + 1] = jnp.zeros_like(act_e[0])
    for edge in (0, nj + 1):
        act_e[pl.ds(1, ni), :, pl.ds(edge * LANES, LANES)] = jnp.zeros((ni, cin, LANES), jnp.bfloat16)
    act_in.wait()

    def turn_act(i, carry):
        stage[pl.ds(0, cin * nj)] = act_v[:, i].astype(jnp.float32).reshape(cin * nj, LANES)
        for j in range(nj):
            act_e[i + 1, :, pl.ds((j + 1) * LANES, LANES)] = stage[pl.ds(j, cin, stride=nj)].astype(jnp.bfloat16)
        return carry

    lax.fori_loop(0, ni, turn_act, 0)
    pl.semaphore_wait(barrier, len(near))
    for n in (4, 5, 6, 7, 2, 3, 0, 1):
        act_halo(n).start()
    tell()

    og_in.wait()

    def turn_og(i, carry):
        stage[...] = og_v[:, i].astype(jnp.float32).reshape(cout * nj, LANES)
        for j in range(nj):
            rows = stage[pl.ds(j, cout, stride=nj)]
            at = pl.ds(j * LANES, LANES)
            og_e[i + 1, :, pl.ds((j + 1) * LANES, LANES)] = rows.astype(jnp.bfloat16)
            og_r[i, pl.ds(0, cout), at] = pltpu.roll(rows, LANES - 1, 1).astype(jnp.bfloat16)
            og_r[i, pl.ds(cout, cout), at] = rows.astype(jnp.bfloat16)
            og_r[i, pl.ds(2 * cout, cout), at] = pltpu.roll(rows, 1, 1).astype(jnp.bfloat16)
        return carry

    lax.fori_loop(0, ni, turn_og, 0)

    def product(taps, cells):
        return lax.dot_general(taps, cells, (((1,), (1,)), ((), ())), preferred_element_type=jnp.float32)

    def weight_term(i):
        taps = jnp.concatenate(
            [act_e[i + a, :, pl.ds(b * LANES, nj * LANES)] for a in range(3) for b in range(3)], axis=0
        )
        return product(taps, og_r[i])

    grad[...] = weight_term(0)
    for i in range(1, ni):
        grad[...] += weight_term(i)

    for n in range(2):
        act_halo(n).wait_recv()
    act_e[ni + 1, :, pl.ds(LANES, nj * LANES)] = land_x[0]
    act_e[0, :, pl.ds(LANES, nj * LANES)] = land_x[1]
    for a, outer, inner in ((0, 0, 0), (2, ni + 1, ni - 1)):
        taps = jnp.concatenate([act_e[outer, :, pl.ds(b * LANES, nj * LANES)] for b in range(3)], axis=0)
        grad[pl.ds(a * 3 * cin, 3 * cin)] += product(taps, og_r[inner])
    for n in range(2, 4):
        act_halo(n).wait_recv()
    act_e[pl.ds(1, ni), :, pl.ds((nj + 1) * LANES, LANES)] = land_y[0]
    act_e[pl.ds(1, ni), :, pl.ds(0, LANES)] = land_y[1]
    for n in range(4, 8):
        act_halo(n).wait_recv()
        di, dj = AROUND[n]
        act_e[ni + 1 if di < 0 else 0, :, pl.ds((nj + 1 if dj < 0 else 0) * LANES, LANES)] = land_c[n - 4]
    for b, outer, inner in ((0, 0, 0), (2, nj + 1, nj - 1)):
        taps = jnp.concatenate(
            [
                jnp.concatenate([act_e[i + a, :, pl.ds(outer * LANES, LANES)] for i in range(ni)], axis=1)
                for a in range(3)
            ],
            axis=0,
        )
        cells = jnp.concatenate([og_r[i, :, pl.ds(inner * LANES, LANES)] for i in range(ni)], axis=1)
        term = product(taps, cells)
        for a in range(3):
            grad[pl.ds((3 * a + b) * cin, cin)] += term[a * cin : (a + 1) * cin]
    tall = 9 * cin
    half = tall // 2
    dense[pl.ds(tall, half)] = jnp.concatenate([grad[:half, LANES:], grad[half:, LANES:]], axis=1)
    part = slots.shape[2]
    extra = 2 * group * part - tall - half
    if extra:
        dense[pl.ds(tall + half, extra)] = jnp.zeros((extra, LANES), jnp.float32)
    for s in range(2 * group):
        if (s + 1) * part <= tall:
            slots[s // group, s % group] = grad[pl.ds(s * part, part), pl.ds(0, LANES)]
            continue
        if s * part < tall:
            dense[pl.ds(s * part, tall - s * part)] = grad[pl.ds(s * part, tall - s * part), pl.ds(0, LANES)]
        slots[s // group, s % group] = dense[pl.ds(s * part, part)]

    def forward(i):
        for p in range(nj // 2):
            taps = jnp.concatenate(
                [
                    act_e[i + a, :, pl.ds((2 * p + b) * LANES, 2 * LANES)]
                    for a in range(3)
                    for b in range(3)
                ],
                axis=0,
            )
            y = jnp.dot(w_fwd[...], taps, preferred_element_type=jnp.float32)
            for q in range(2):
                t = y[:, q * LANES : (q + 1) * LANES]
                total = t[cout : 2 * cout] + pltpu.roll(t[:cout], 1, 1) + pltpu.roll(t[2 * cout :], LANES - 1, 1)
                stage[pl.ds(2 * p + q, cout, stride=nj)] = total
        out_v[i] = stage[...].astype(jnp.bfloat16).reshape(cout, nj, LANES)
        pltpu.make_async_copy(out_v.at[i], out_hbm.at[:, i], out_sem.at[i]).start()

    def backward(i):
        for p in range(nj // 2):
            taps = jnp.concatenate(
                [
                    og_e[i + 2 - a, :, pl.ds((2 * p + 2 - b) * LANES, 2 * LANES)]
                    for a in range(3)
                    for b in range(3)
                ],
                axis=0,
            )
            y = jnp.dot(w_bwd[...], taps, preferred_element_type=jnp.float32)
            for q in range(2):
                t = y[:, q * LANES : (q + 1) * LANES]
                total = t[cin : 2 * cin] + pltpu.roll(t[:cin], LANES - 1, 1) + pltpu.roll(t[2 * cin :], 1, 1)
                stage[pl.ds(2 * p + q, cin, stride=nj)] = total
        ing_v[i] = stage[pl.ds(0, cin * nj)].astype(jnp.bfloat16).reshape(cin, nj, LANES)
        pltpu.make_async_copy(ing_v.at[i], ing_hbm.at[:, i], out_sem.at[ni + i]).start()

    def to_group(q):
        d, flip = q // 2, q % 2
        return pltpu.make_async_remote_copy(
            src_ref=slots.at[core + flip * (1 - 2 * core), place_across(d)], dst_ref=parts.at[core, place],
            send_sem=p1_send.at[q], recv_sem=p1_recv.at[q], device_id=across(d, flip), device_id_type=MESH)

    def to_z(dz):
        return pltpu.make_async_remote_copy(
            src_ref=lifted.at[z], dst_ref=lifted.at[z], send_sem=p2_send.at[dz], recv_sem=p2_recv.at[dz],
            device_id=along_z(dz), device_id_type=MESH)

    def back_group(q):
        return pltpu.make_async_remote_copy(
            src_ref=mine, dst_ref=full.at[core, place], send_sem=p3_send.at[q], recv_sem=p3_recv.at[q],
            device_id=across(q // 2, q % 2), device_id_type=MESH)

    own = pltpu.make_async_copy(mine, full.at[core, place], mine_sem.at[0])

    def each(low, high, do):
        def body(t, carry):
            do(t)
            return carry

        lax.fori_loop(low, high, body, 0)

    pl.semaphore_wait(seen, 4)
    for q in far_first:
        to_group(q).start()
    parts[core, place] = slots[core, place]
    for n in range(2):
        halo(og_e, n, ho_send, ho_recv).start()
    w_in.wait()
    w = w_v[...].astype(jnp.float32).reshape(9, 3, cin, cout)
    by_tap = jnp.concatenate([w[:, e].reshape(9 * cin, cout) for e in range(3)], axis=1)
    w_fwd[...] = by_tap.T.astype(jnp.bfloat16)
    w_bwd[...] = jnp.concatenate([w[n].reshape(3 * cin, cout) for n in range(9)], axis=1).astype(jnp.bfloat16)
    each(0, 2, forward)
    each(1, peers, lambda q: to_group(q).wait_recv())
    lifted[z] = jnp.sum(parts[...], axis=(0, 1))
    each(1, nz, lambda dz: to_z(dz).start())
    for n in range(2, 8):
        halo(og_e, n, ho_send, ho_recv).start()
    each(2, ni, forward)
    each(1, nz, lambda dz: to_z(dz).wait_recv())
    mine[...] = jnp.sum(lifted[...], axis=0) * jnp.float32(scale)
    for q in far_first:
        back_group(q).start()
    own.start()
    for n in range(8):
        halo(og_e, n, ho_send, ho_recv).wait_recv()
    each(0, ni, backward)


    for n in range(8):
        act_halo(n).wait_send()
        halo(og_e, n, ho_send, ho_recv).wait_send()
    each(1, peers, lambda q: to_group(q).wait_send())
    each(1, nz, lambda dz: to_z(dz).wait_send())
    each(1, peers, lambda q: back_group(q).wait_send())
    each(0, ni, lambda i: pltpu.make_async_copy(out_v.at[i], out_hbm.at[:, i], out_sem.at[i]).wait())
    each(0, ni, lambda i: pltpu.make_async_copy(ing_v.at[i], ing_hbm.at[:, i], out_sem.at[ni + i]).wait())
    own.wait()
    each(1, peers, lambda q: back_group(q).wait_recv())


def deliver(cin, cout, out_v, ing_v, full, out_hbm, ing_hbm, kg_hbm, dense, kg_v, sem):
    piece = cin // 2
    pairs = [(out_v, out_hbm, n) for n in range(0, cout, piece)] + [(ing_v, ing_hbm, n) for n in range(0, cin, piece)]
    copies = [
        pltpu.make_async_copy(source.at[pl.ds(n, piece)], target.at[pl.ds(n, piece)], sem.at[m])
        for m, (source, target, n) in enumerate(pairs)
    ]
    for copy in copies:
        copy.start()
    last = pltpu.make_async_copy(kg_v, kg_hbm, sem.at[len(pairs)])
    _, group, part, _ = full.shape
    tall = 9 * cin
    half = tall // 2
    for s in range(2 * group):
        dense[pl.ds(s * part, part)] = full[s // group, s % group]
    for n in range(9):
        rows = pl.ds(n * cin, cin)
        kg_v[pl.ds(n * 3 * cin, cin)] = dense[rows, pl.ds(0, cout)]
        kg_v[pl.ds((n * 3 + 1) * cin, cin)] = dense[rows, pl.ds(cout, cout)]
    third = jnp.concatenate([dense[pl.ds(tall, half), :cout], dense[pl.ds(tall, half), cout:]], axis=0)
    for n in range(9):
        kg_v[pl.ds((n * 3 + 2) * cin, cin)] = third[n * cin : (n + 1) * cin]
    last.start()
    for copy in copies:
        copy.wait()
    last.wait()


def local(sizes, activations, weights, out_grad):
    n_dp, n_gx, n_gy = sizes
    univ, cin, ni, nj, nk = activations.shape
    cout = out_grad.shape[1]
    nz, group = n_gx // 2, n_dp * n_gy
    scale = 1.0 / math.sqrt(univ * n_dp * ni * n_gx * nj * n_gy * nk)
    part = -(-27 * cin * cout // (LANES * 2 * group))
    bf16, f32 = jnp.bfloat16, jnp.float32
    dma = pltpu.SemaphoreType.DMA
    taps = weights.transpose(2, 3, 4, 1, 0).reshape(27 * cin, cout)
    output, in_grad, gathered = pl.pallas_call(
        functools.partial(kernel, sizes, scale),
        out_shape=(
            jax.ShapeDtypeStruct((cout, ni, nj, nk), bf16),
            jax.ShapeDtypeStruct((cin, ni, nj, nk), bf16),
            jax.ShapeDtypeStruct((2, group, part, LANES), f32),
        ),
        in_specs=[
            pl.BlockSpec(memory_space=pltpu.HBM),
            pl.BlockSpec(memory_space=pltpu.HBM),
            pl.BlockSpec(memory_space=pltpu.HBM),
        ],
        out_specs=(
            pl.BlockSpec(memory_space=pl.ANY),
            pl.BlockSpec(memory_space=pl.ANY),
            pl.BlockSpec(memory_space=pl.ANY),
        ),
        scratch_shapes=[
            pltpu.VMEM((cin, ni, nj, nk), bf16),
            pltpu.VMEM((27 * cin, cout), bf16),
            pltpu.VMEM((cout, ni, nj, nk), bf16),
            pltpu.VMEM((ni + 2, cin, (nj + 2) * nk), bf16),
            pltpu.VMEM((ni + 2, cout, (nj + 2) * nk), bf16),
            pltpu.VMEM((ni, 3 * cout, nj * nk), bf16),
            pltpu.VMEM((2, cin, nj * nk), bf16),
            pltpu.VMEM((2, ni, cin, nk), bf16),
            pltpu.VMEM((4, cin, nk), bf16),
            pltpu.VMEM((cout * nj, nk), f32),
            pltpu.VMEM((3 * cout, 9 * cin), bf16),
            pltpu.VMEM((3 * cin, 9 * cout), bf16),
            pltpu.VMEM((9 * cin, 3 * cout), f32),
            pltpu.VMEM((2 * group * part, LANES), f32),
            pltpu.VMEM((2, group, part, LANES), f32),
            pltpu.VMEM((2, group, part, LANES), f32),
            pltpu.VMEM((nz, part, LANES), f32),
            pltpu.VMEM((part, LANES), f32),
            pltpu.VMEM((ni, cout, nj, nk), bf16),
            pltpu.VMEM((ni, cin, nj, nk), bf16),
            dma((3,)),
            dma((2 * ni,)),
            dma((8,)), dma((8,)), dma((8,)), dma((8,)),
            dma((2 * group,)), dma((2 * group,)),
            dma((nz,)), dma((nz,)),
            dma((2 * group,)), dma((2 * group,)),
            dma((1,)),
            pltpu.SemaphoreType.REGULAR,
        ],
        compiler_params=pltpu.CompilerParams(
            collective_id=0, has_side_effects=True, vmem_limit_bytes=48 * 1024 * 1024
        ),
        cost_estimate=pl.CostEstimate(flops=3_000_000_000, bytes_accessed=4_000_000, transcendentals=0),
    )(*(pltpu.with_memory_space_constraint(x, pltpu.HBM) for x in (activations[0], taps, out_grad[0])))
    held = tuple(pltpu.with_memory_space_constraint(x, pltpu.VMEM) for x in (output, in_grad, gathered))
    output, in_grad, kernel_grad = pl.pallas_call(
        functools.partial(deliver, cin, cout),
        out_shape=(
            jax.ShapeDtypeStruct(output.shape, bf16),
            jax.ShapeDtypeStruct(in_grad.shape, bf16),
            jax.ShapeDtypeStruct((27 * cin, cout), f32),
        ),
        in_specs=[pl.BlockSpec(memory_space=pltpu.VMEM)] * 3,
        out_specs=(pl.BlockSpec(memory_space=pltpu.HBM),) * 3,
        scratch_shapes=[
            pltpu.VMEM((2 * group * part, LANES), f32),
            pltpu.VMEM((27 * cin, cout), f32),
            dma((2 * cout // cin + 3,)),
        ],
    )(*held)
    kernel_grad = kernel_grad.reshape(3, 3, 3, cin, cout).transpose(4, 3, 0, 1, 2)
    return (output[None], in_grad[None], kernel_grad)


def solution(mesh):
    sizes = (mesh.shape["dp"], mesh.shape["gx"], mesh.shape["gy"])
    return jax.shard_map(
        functools.partial(local, sizes),
        mesh=mesh,
        in_specs=(P("dp", None, "gx", "gy", None), P(), P("dp", None, "gx", "gy", None)),
        out_specs=(P("dp", None, "gx", "gy", None), P("dp", None, "gx", "gy", None), P()),
        check_vma=False,
    )
```

```python
import functools
import math

import jax
import jax.numpy as jnp
from jax import lax
from jax.experimental import pallas as pl
from jax.experimental.pallas import tpu as pltpu
from jax.sharding import PartitionSpec as P

MESH = pl.DeviceIdType.MESH
LANES = 128
AROUND = [(-1, 0), (1, 0), (0, -1), (0, 1), (-1, -1), (-1, 1), (1, -1), (1, 1)]


def kernel(sizes, scale, act_hbm, w_hbm, og_hbm, out_hbm, ing_hbm, full,
           act_v, w_v, og_v, act_e, og_e, og_r, land_x, land_y, land_c, stage, w_fwd, w_bwd, grad, dense, slots, parts, lifted, mine,
           out_v, ing_v, in_sem, out_sem, ha_send, ha_recv, ho_send, ho_recv,
           p1_send, p1_recv, p2_send, p2_recv, p3_send, p3_recv, mine_sem, seen):
    n_dp, n_gx, n_gy = sizes
    cin, ni, nj, _ = act_v.shape
    cout = og_v.shape[0]
    nz = n_gx // 2
    group = n_dp * n_gy
    dp, gx, gy = lax.axis_index("dp"), lax.axis_index("gx"), lax.axis_index("gy")
    z, core = lax.div(gx, 2), lax.rem(gx, 2)
    place = dp * n_gy + gy

    def shifted(di, dj):
        return (dp, lax.rem(gx + di + n_gx, n_gx), lax.rem(gy + dj + n_gy, n_gy))

    def along_z(dz):
        return (dp, lax.rem(z + dz + nz, nz) * 2 + core, gy)

    def across(d, flip=0):
        return (
            lax.rem(dp + d // n_gy, n_dp),
            z * 2 + core + flip * (1 - 2 * core),
            lax.rem(gy + d % n_gy, n_gy),
        )

    def place_across(d):
        return lax.rem(dp + d // n_gy, n_dp) * n_gy + lax.rem(gy + d % n_gy, n_gy)

    act_in = pltpu.make_async_copy(act_hbm, act_v, in_sem.at[0])
    og_in = pltpu.make_async_copy(og_hbm, og_v, in_sem.at[1])
    w_in = pltpu.make_async_copy(w_hbm, w_v, in_sem.at[2])
    act_in.start()
    og_in.start()
    w_in.start()

    barrier = pltpu.get_barrier_semaphore()

    def greet(target):
        pl.semaphore_signal(barrier, inc=1, device_id=target, device_id_type=MESH)

    def hops(d):
        far_y = d % n_gy
        return min(far_y, n_gy - far_y) / 2 + (1.5 if far_y % 2 else 2 * (d // n_gy))

    peers = 2 * group
    far_first = sorted(range(1, peers), key=lambda q: -hops(q // 2))
    near = [(hops(d), across(d, flip)) for d in range(2, group) for flip in range(2) if d != n_gy - 1 and hops(d) <= 2]
    near += [(d, along_z(way * d)) for d in range(1, min(nz, 3)) for way in (1, -1)]
    near += [(abs(di) + 1.5 * abs(dj), shifted(di, dj)) for di, dj in AROUND]
    for _, target in sorted(near, key=lambda t: -t[0]):
        greet(target)

    def tell():
        for target in (across(n_gy % group), across(n_gy // 2), along_z(2), along_z(-2)):
            pl.semaphore_signal(seen, inc=1, device_id=target, device_id_type=MESH)

    def halo(field, n, send, recv, landing=None):
        di, dj = AROUND[n]
        rows = {-1: (1, ni + 1, 1), 0: (1, 1, ni), 1: (ni, 0, 1)}[di]
        cols = {-1: (1, nj + 1, 1), 0: (1, 1, nj), 1: (nj, 0, 1)}[dj]
        if landing is None:
            landing = field.at[pl.ds(rows[1], rows[2]), :, pl.ds(cols[1] * LANES, cols[2] * LANES)]
        return pltpu.make_async_remote_copy(
            src_ref=field.at[pl.ds(rows[0], rows[2]), :, pl.ds(cols[0] * LANES, cols[2] * LANES)],
            dst_ref=landing,
            send_sem=send.at[n],
            recv_sem=recv.at[n],
            device_id=shifted(di, dj),
            device_id_type=MESH,
        )

    def act_halo(n):
        if n < 2:
            landing = land_x.at[pl.ds(n, 1)]
        elif n < 4:
            landing = land_y.at[n - 2]
        else:
            landing = land_c.at[pl.ds(n - 4, 1)]
        return halo(act_e, n, ha_send, ha_recv, landing)

    act_e[0] = jnp.zeros_like(act_e[0])
    act_e[ni + 1] = jnp.zeros_like(act_e[0])
    for edge in (0, nj + 1):
        act_e[pl.ds(1, ni), :, pl.ds(edge * LANES, LANES)] = jnp.zeros((ni, cin, LANES), jnp.bfloat16)
    act_in.wait()

    def turn_act(i, carry):
        stage[pl.ds(0, cin * nj)] = act_v[:, i].astype(jnp.float32).reshape(cin * nj, LANES)
        for j in range(nj):
            act_e[i + 1, :, pl.ds((j + 1) * LANES, LANES)] = stage[pl.ds(j, cin, stride=nj)].astype(jnp.bfloat16)
        return carry

    lax.fori_loop(0, ni, turn_act, 0)
    pl.semaphore_wait(barrier, len(near))
    tell()
    for n in (4, 5, 6, 7, 2, 3, 0, 1):
        act_halo(n).start()

    og_in.wait()

    def turn_og(i, carry):
        stage[...] = og_v[:, i].astype(jnp.float32).reshape(cout * nj, LANES)
        for j in range(nj):
            rows = stage[pl.ds(j, cout, stride=nj)]
            at = pl.ds(j * LANES, LANES)
            og_e[i + 1, :, pl.ds((j + 1) * LANES, LANES)] = rows.astype(jnp.bfloat16)
            og_r[i, pl.ds(0, cout), at] = pltpu.roll(rows, LANES - 1, 1).astype(jnp.bfloat16)
            og_r[i, pl.ds(cout, cout), at] = rows.astype(jnp.bfloat16)
            og_r[i, pl.ds(2 * cout, cout), at] = pltpu.roll(rows, 1, 1).astype(jnp.bfloat16)
        return carry

    lax.fori_loop(0, ni, turn_og, 0)

    def product(taps, cells):
        return lax.dot_general(taps, cells, (((1,), (1,)), ((), ())), preferred_element_type=jnp.float32)

    def weight_term(i):
        taps = jnp.concatenate(
            [act_e[i + a, :, pl.ds(b * LANES, nj * LANES)] for a in range(3) for b in range(3)], axis=0
        )
        return product(taps, og_r[i])

    grad[...] = weight_term(0)
    for i in range(1, ni):
        grad[...] += weight_term(i)

    for n in range(2):
        act_halo(n).wait_recv()
    act_e[ni + 1, :, pl.ds(LANES, nj * LANES)] = land_x[0]
    act_e[0, :, pl.ds(LANES, nj * LANES)] = land_x[1]
    for a, outer, inner in ((0, 0, 0), (2, ni + 1, ni - 1)):
        taps = jnp.concatenate([act_e[outer, :, pl.ds(b * LANES, nj * LANES)] for b in range(3)], axis=0)
        grad[pl.ds(a * 3 * cin, 3 * cin)] += product(taps, og_r[inner])
    for n in range(2, 4):
        act_halo(n).wait_recv()
    act_e[pl.ds(1, ni), :, pl.ds((nj + 1) * LANES, LANES)] = land_y[0]
    act_e[pl.ds(1, ni), :, pl.ds(0, LANES)] = land_y[1]
    for n in range(4, 8):
        act_halo(n).wait_recv()
        di, dj = AROUND[n]
        act_e[ni + 1 if di < 0 else 0, :, pl.ds((nj + 1 if dj < 0 else 0) * LANES, LANES)] = land_c[n - 4]
    for b, outer, inner in ((0, 0, 0), (2, nj + 1, nj - 1)):
        taps = jnp.concatenate(
            [
                jnp.concatenate([act_e[i + a, :, pl.ds(outer * LANES, LANES)] for i in range(ni)], axis=1)
                for a in range(3)
            ],
            axis=0,
        )
        cells = jnp.concatenate([og_r[i, :, pl.ds(inner * LANES, LANES)] for i in range(ni)], axis=1)
        term = product(taps, cells)
        for a in range(3):
            grad[pl.ds((3 * a + b) * cin, cin)] += term[a * cin : (a + 1) * cin]
    tall = 9 * cin
    half = tall // 2
    dense[pl.ds(tall, half)] = jnp.concatenate([grad[:half, LANES:], grad[half:, LANES:]], axis=1)
    part = slots.shape[2]
    extra = 2 * group * part - tall - half
    if extra:
        dense[pl.ds(tall + half, extra)] = jnp.zeros((extra, LANES), jnp.float32)
    for s in range(2 * group):
        if (s + 1) * part <= tall:
            slots[s // group, s % group] = grad[pl.ds(s * part, part), pl.ds(0, LANES)]
            continue
        if s * part < tall:
            dense[pl.ds(s * part, tall - s * part)] = grad[pl.ds(s * part, tall - s * part), pl.ds(0, LANES)]
        slots[s // group, s % group] = dense[pl.ds(s * part, part)]

    def forward(i):
        for p in range(nj // 2):
            taps = jnp.concatenate(
                [
                    act_e[i + a, :, pl.ds((2 * p + b) * LANES, 2 * LANES)]
                    for a in range(3)
                    for b in range(3)
                ],
                axis=0,
            )
            y = jnp.dot(w_fwd[...], taps, preferred_element_type=jnp.float32)
            for q in range(2):
                t = y[:, q * LANES : (q + 1) * LANES]
                total = t[cout : 2 * cout] + pltpu.roll(t[:cout], 1, 1) + pltpu.roll(t[2 * cout :], LANES - 1, 1)
                stage[pl.ds(2 * p + q, cout, stride=nj)] = total
        out_v[i] = stage[...].astype(jnp.bfloat16).reshape(cout, nj, LANES)
        pltpu.make_async_copy(out_v.at[i], out_hbm.at[:, i], out_sem.at[i]).start()

    def backward(i):
        for p in range(nj // 2):
            taps = jnp.concatenate(
                [
                    og_e[i + 2 - a, :, pl.ds((2 * p + 2 - b) * LANES, 2 * LANES)]
                    for a in range(3)
                    for b in range(3)
                ],
                axis=0,
            )
            y = jnp.dot(w_bwd[...], taps, preferred_element_type=jnp.float32)
            for q in range(2):
                t = y[:, q * LANES : (q + 1) * LANES]
                total = t[cin : 2 * cin] + pltpu.roll(t[:cin], LANES - 1, 1) + pltpu.roll(t[2 * cin :], 1, 1)
                stage[pl.ds(2 * p + q, cin, stride=nj)] = total
        ing_v[i] = stage[pl.ds(0, cin * nj)].astype(jnp.bfloat16).reshape(cin, nj, LANES)
        pltpu.make_async_copy(ing_v.at[i], ing_hbm.at[:, i], out_sem.at[ni + i]).start()

    def to_group(q):
        d, flip = q // 2, q % 2
        return pltpu.make_async_remote_copy(
            src_ref=slots.at[core + flip * (1 - 2 * core), place_across(d)], dst_ref=parts.at[core, place],
            send_sem=p1_send.at[q], recv_sem=p1_recv.at[q], device_id=across(d, flip), device_id_type=MESH)

    def to_z(dz):
        return pltpu.make_async_remote_copy(
            src_ref=lifted.at[z], dst_ref=lifted.at[z], send_sem=p2_send.at[dz], recv_sem=p2_recv.at[dz],
            device_id=along_z(dz), device_id_type=MESH)

    def back_group(q):
        return pltpu.make_async_remote_copy(
            src_ref=mine, dst_ref=full.at[core, place], send_sem=p3_send.at[q], recv_sem=p3_recv.at[q],
            device_id=across(q // 2, q % 2), device_id_type=MESH)

    own = pltpu.make_async_copy(mine, full.at[core, place], mine_sem.at[0])

    def each(low, high, do):
        def body(t, carry):
            do(t)
            return carry

        lax.fori_loop(low, high, body, 0)

    pl.semaphore_wait(seen, 4)
    for q in far_first:
        to_group(q).start()
    parts[core, place] = slots[core, place]
    for n in range(2):
        halo(og_e, n, ho_send, ho_recv).start()
    w_in.wait()
    w = w_v[...].astype(jnp.float32).reshape(9, 3, cin, cout)
    by_tap = jnp.concatenate([w[:, e].reshape(9 * cin, cout) for e in range(3)], axis=1)
    w_fwd[...] = by_tap.T.astype(jnp.bfloat16)
    w_bwd[...] = jnp.concatenate([w[n].reshape(3 * cin, cout) for n in range(9)], axis=1).astype(jnp.bfloat16)
    each(0, 2, forward)
    for q in reversed(far_first):
        to_group(q).wait_recv()
    lifted[z] = jnp.sum(parts[...], axis=(0, 1))
    for dz in sorted(range(1, nz), key=lambda d: -min(d, nz - d)):
        to_z(dz).start()
    for n in range(2, 8):
        halo(og_e, n, ho_send, ho_recv).start()
    each(2, ni, forward)
    for dz in sorted(range(1, nz), key=lambda d: min(d, nz - d)):
        to_z(dz).wait_recv()
    mine[...] = jnp.sum(lifted[...], axis=0) * jnp.float32(scale)
    for q in far_first:
        back_group(q).start()
    own.start()
    for n in range(8):
        halo(og_e, n, ho_send, ho_recv).wait_recv()
    each(0, ni, backward)


    for n in range(8):
        act_halo(n).wait_send()
        halo(og_e, n, ho_send, ho_recv).wait_send()
    each(1, peers, lambda q: to_group(q).wait_send())
    each(1, nz, lambda dz: to_z(dz).wait_send())
    each(1, peers, lambda q: back_group(q).wait_send())
    each(0, ni, lambda i: pltpu.make_async_copy(out_v.at[i], out_hbm.at[:, i], out_sem.at[i]).wait())
    each(0, ni, lambda i: pltpu.make_async_copy(ing_v.at[i], ing_hbm.at[:, i], out_sem.at[ni + i]).wait())
    own.wait()
    for q in reversed(far_first):
        back_group(q).wait_recv()


def deliver(cin, cout, out_v, ing_v, full, out_hbm, ing_hbm, kg_hbm, dense, kg_v, sem):
    piece = cin // 2
    pairs = [(out_v, out_hbm, n) for n in range(0, cout, piece)] + [(ing_v, ing_hbm, n) for n in range(0, cin, piece)]
    copies = [
        pltpu.make_async_copy(source.at[pl.ds(n, piece)], target.at[pl.ds(n, piece)], sem.at[m])
        for m, (source, target, n) in enumerate(pairs)
    ]
    for copy in copies:
        copy.start()
    last = pltpu.make_async_copy(kg_v, kg_hbm, sem.at[len(pairs)])
    _, group, part, _ = full.shape
    tall = 9 * cin
    half = tall // 2
    for s in range(2 * group):
        dense[pl.ds(s * part, part)] = full[s // group, s % group]
    for n in range(9):
        rows = pl.ds(n * cin, cin)
        kg_v[pl.ds(n * 3 * cin, cin)] = dense[rows, pl.ds(0, cout)]
        kg_v[pl.ds((n * 3 + 1) * cin, cin)] = dense[rows, pl.ds(cout, cout)]
    third = jnp.concatenate([dense[pl.ds(tall, half), :cout], dense[pl.ds(tall, half), cout:]], axis=0)
    for n in range(9):
        kg_v[pl.ds((n * 3 + 2) * cin, cin)] = third[n * cin : (n + 1) * cin]
    last.start()
    for copy in copies:
        copy.wait()
    last.wait()


def local(sizes, activations, weights, out_grad):
    n_dp, n_gx, n_gy = sizes
    univ, cin, ni, nj, nk = activations.shape
    cout = out_grad.shape[1]
    nz, group = n_gx // 2, n_dp * n_gy
    scale = 1.0 / math.sqrt(univ * n_dp * ni * n_gx * nj * n_gy * nk)
    part = -(-27 * cin * cout // (LANES * 2 * group))
    bf16, f32 = jnp.bfloat16, jnp.float32
    dma = pltpu.SemaphoreType.DMA
    taps = weights.transpose(2, 3, 4, 1, 0).reshape(27 * cin, cout)
    output, in_grad, gathered = pl.pallas_call(
        functools.partial(kernel, sizes, scale),
        out_shape=(
            jax.ShapeDtypeStruct((cout, ni, nj, nk), bf16),
            jax.ShapeDtypeStruct((cin, ni, nj, nk), bf16),
            jax.ShapeDtypeStruct((2, group, part, LANES), f32),
        ),
        in_specs=[
            pl.BlockSpec(memory_space=pltpu.HBM),
            pl.BlockSpec(memory_space=pltpu.HBM),
            pl.BlockSpec(memory_space=pltpu.HBM),
        ],
        out_specs=(
            pl.BlockSpec(memory_space=pl.ANY),
            pl.BlockSpec(memory_space=pl.ANY),
            pl.BlockSpec(memory_space=pl.ANY),
        ),
        scratch_shapes=[
            pltpu.VMEM((cin, ni, nj, nk), bf16),
            pltpu.VMEM((27 * cin, cout), bf16),
            pltpu.VMEM((cout, ni, nj, nk), bf16),
            pltpu.VMEM((ni + 2, cin, (nj + 2) * nk), bf16),
            pltpu.VMEM((ni + 2, cout, (nj + 2) * nk), bf16),
            pltpu.VMEM((ni, 3 * cout, nj * nk), bf16),
            pltpu.VMEM((2, cin, nj * nk), bf16),
            pltpu.VMEM((2, ni, cin, nk), bf16),
            pltpu.VMEM((4, cin, nk), bf16),
            pltpu.VMEM((cout * nj, nk), f32),
            pltpu.VMEM((3 * cout, 9 * cin), bf16),
            pltpu.VMEM((3 * cin, 9 * cout), bf16),
            pltpu.VMEM((9 * cin, 3 * cout), f32),
            pltpu.VMEM((2 * group * part, LANES), f32),
            pltpu.VMEM((2, group, part, LANES), f32),
            pltpu.VMEM((2, group, part, LANES), f32),
            pltpu.VMEM((nz, part, LANES), f32),
            pltpu.VMEM((part, LANES), f32),
            pltpu.VMEM((ni, cout, nj, nk), bf16),
            pltpu.VMEM((ni, cin, nj, nk), bf16),
            dma((3,)),
            dma((2 * ni,)),
            dma((8,)), dma((8,)), dma((8,)), dma((8,)),
            dma((2 * group,)), dma((2 * group,)),
            dma((nz,)), dma((nz,)),
            dma((2 * group,)), dma((2 * group,)),
            dma((1,)),
            pltpu.SemaphoreType.REGULAR,
        ],
        compiler_params=pltpu.CompilerParams(
            collective_id=0, has_side_effects=True, vmem_limit_bytes=48 * 1024 * 1024
        ),
        cost_estimate=pl.CostEstimate(flops=3_000_000_000, bytes_accessed=4_000_000, transcendentals=0),
    )(*(pltpu.with_memory_space_constraint(x, pltpu.HBM) for x in (activations[0], taps, out_grad[0])))
    held = tuple(pltpu.with_memory_space_constraint(x, pltpu.VMEM) for x in (output, in_grad, gathered))
    output, in_grad, kernel_grad = pl.pallas_call(
        functools.partial(deliver, cin, cout),
        out_shape=(
            jax.ShapeDtypeStruct(output.shape, bf16),
            jax.ShapeDtypeStruct(in_grad.shape, bf16),
            jax.ShapeDtypeStruct((27 * cin, cout), f32),
        ),
        in_specs=[pl.BlockSpec(memory_space=pltpu.VMEM)] * 3,
        out_specs=(pl.BlockSpec(memory_space=pltpu.HBM),) * 3,
        scratch_shapes=[
            pltpu.VMEM((2 * group * part, LANES), f32),
            pltpu.VMEM((27 * cin, cout), f32),
            dma((2 * cout // cin + 3,)),
        ],
    )(*held)
    kernel_grad = kernel_grad.reshape(3, 3, 3, cin, cout).transpose(4, 3, 0, 1, 2)
    return (output[None], in_grad[None], kernel_grad)


def solution(mesh):
    sizes = (mesh.shape["dp"], mesh.shape["gx"], mesh.shape["gy"])
    return jax.shard_map(
        functools.partial(local, sizes),
        mesh=mesh,
        in_specs=(P("dp", None, "gx", "gy", None), P(), P("dp", None, "gx", "gy", None)),
        out_specs=(P("dp", None, "gx", "gy", None), P("dp", None, "gx", "gy", None), P()),
        check_vma=False,
    )
```
